128 devices in a mesh: sub: 32 (over y, x, core), grp: 4 (over z).
Axes of the slice: x: 4, y: 4, z: 4, core: 2. Of those that a mesh axis runs over, the one named last changes fastest.
Arguments:
- right_side: float32 [4096, 256, 128], P(('sub', 'grp')), may hold values from -13 to 13
- diag_blocks: float32 [4096, 128, 128], P(('sub', 'grp')), may hold values from -1 to 5.5, as said below
- couplings: float32 [4096, 4, 128, 128], P(('sub', 'grp')), may hold values from -0.25 to 0.25
- factors: float32 [4096, 128, 128], P(('sub', 'grp')), may hold values from -1 to 1, as said below
- prolong: float32 [4096, 8, 128], P(('sub', 'grp')), may hold values from -1.5 to 1.5
- coarse_inverse: float32 [32, 1024, 1024], P('sub', 'grp'), may hold values from -1 to 1, as said below
- intersection_send: int32 [512], P(('sub', 'grp')), may hold values from 0 to 31, as said below
- neighbours: int32 [4096, 4], P(('sub', 'grp')), may hold values from 0 to 39, as said below
- coarse_pick: int32 [4096], P(('sub', 'grp')), may hold values from 0 to 31, as said below
Outputs:
- solution: float32 [4096, 256, 128], P(('sub', 'grp'))
- residual: float32 [4096, 256, 128], P(('sub', 'grp'))
The draws below stay inside these ranges and needn't reach their ends.
Inputs may be any that keep to these rules, and one draw needn't show every extreme that they name: `neighbours`: block rows of one device name entries of that device's ext: its 32 own blocks first, then the 4 received from the lower neighbour, then the 4 from the upper one; on every device each of the 8 received blocks is named by some entry. `intersection_send`: each device's 4 entries are distinct local block numbers. `coarse_pick`: each device's 32 entries form a permutation of its local block numbers. `diag_blocks`: diagonal entries lie in 3.5 to 5.5; each off-diagonal entry is at most 1.8 / 128**0.5 in magnitude. `factors`: diagonal entries lie in 0.45 to 0.75; each off-diagonal entry is at most 0.3 / 128**0.5 in magnitude. `coarse_inverse`: diagonal entries lie in 0.3 to 0.6; each off-diagonal entry is at most 0.3 / 1024**0.5 in magnitude.
All inputs are finite; a program needn't handle non-finite values.
Results may differ from the reference program's by a relative error of at most 0.00026.
Values sent between devices are 32-bit elements; how exact they have to be, the bound alone decides.
No kernel may reach another device: no remote copies, remote signals or barrier semaphores. Data moves between devices by JAX's collectives and lax.ppermute only.
A program may use at most 192 MiB of HBM per device.

```python
import math
import jax
import jax.numpy as jnp
from jax import lax

B = 128
R = 256
BLK_DEV = 32
K = 4
HALO = 4
NCF = 8
ITERS = 3
NBLK = 4096
NSEND = 512
CG = 1024
N_SUB = 32
N_GRP = 4


def draw_right_side(key, part):
    key_rough, key_scale = jax.random.split(key, 2)
    position = jnp.arange(NBLK, dtype=jnp.float32) / max(NBLK - 1, 1)
    rising = 1.0 + 2.0 * position
    scales = jnp.exp(jax.random.uniform(key_scale, (NBLK,), jnp.float32, math.log(0.1), 0.0))
    rough = jax.random.truncated_normal(key_rough, -4.0, 4.0, (NBLK, R, B), jnp.float32)
    return (rough * (rising * scales)[:, None, None]).astype(jnp.float32)


def dominant_blocks(key, count, order, low, high, spread):
    key_diag, key_off = jax.random.split(key, 2)
    eye = jnp.eye(order, dtype=jnp.float32)
    diag = jax.random.uniform(key_diag, (count, 1, order), jnp.float32, low, high)
    off = jax.random.uniform(key_off, (count, order, order), jnp.float32, -1.0, 1.0)
    return eye * diag + (1.0 - eye) * off * (spread / math.sqrt(order))


def draw_diag_blocks(key, part):
    return dominant_blocks(key, NBLK, B, 3.5, 5.5, 1.8)


def draw_factors(key, part):
    return dominant_blocks(key, NBLK, B, 0.45, 0.75, 0.3)


def draw_coarse_inverse(key, part):
    return dominant_blocks(key, N_SUB, CG, 0.3, 0.6, 0.3)


def draw_intersection_send(key, part):
    devices = NSEND // HALO
    keys = jax.random.split(key, devices + 1)
    orders = jax.vmap(lambda one: jax.random.permutation(one, BLK_DEV))(keys[:devices])
    lists = orders[:, :HALO].astype(jnp.int32)
    middle = (1 + jax.random.permutation(keys[devices], BLK_DEV - 2)).astype(jnp.int32)
    first = jnp.concatenate([jnp.array([0, BLK_DEV - 1], jnp.int32), middle[:HALO - 2]])
    lists = lists.at[0].set(first)
    return lists.reshape(NSEND).astype(jnp.int32)


def one_device_pattern(one):
    key_order, key_rest = jax.random.split(one, 2)
    order = jax.random.permutation(key_order, BLK_DEV)
    labels = (BLK_DEV + jnp.arange(BLK_DEV, dtype=jnp.int32) % (2 * HALO)).astype(jnp.int32)
    first = jnp.zeros((BLK_DEV,), jnp.int32).at[order].set(labels)
    others = jax.random.randint(key_rest, (BLK_DEV, K - 1), 0, BLK_DEV + 2 * HALO, jnp.int32)
    return jnp.concatenate([first[:, None], others], axis=1)


def draw_neighbours(key, part):
    devices = NBLK // BLK_DEV
    keys = jax.random.split(key, devices)
    pattern = jax.vmap(one_device_pattern)(keys)
    pattern = pattern.at[0, 0, 1].set(0)
    return pattern.reshape(NBLK, K).astype(jnp.int32)


def draw_coarse_pick(key, part):
    devices = NBLK // BLK_DEV
    keys = jax.random.split(key, devices)
    orders = jax.vmap(lambda one: jax.random.permutation(one, BLK_DEV))(keys)
    return orders.reshape(NBLK).astype(jnp.int32)


def block_scale(rng, shape, cuts, low, top_value):
    def one(dim, parts):
        draws = jax.random.uniform(jax.random.fold_in(jax.random.fold_in(rng, 6), dim), (parts,), jnp.float32, low / len(cuts), top_value / len(cuts))
        return jnp.repeat(jnp.exp(draws), shape[dim] // parts).reshape((-1,) + (1,) * (len(shape) - dim - 1))

    level = one(*cuts[0])
    for cut in cuts[1:]:
        level = level * one(*cut)
    return level


def scatter_about(key, extent, scale, reach, pieces=(), kind=jnp.bfloat16):
    loudness = block_scale(key, extent, pieces, -0.22, 0.18) if pieces else 1.0
    drawn = jax.random.normal(key, extent, jnp.float32) * scale * loudness
    return jnp.minimum(jnp.maximum(drawn, -reach), reach).astype(kind)


def setup_inputs(seed: int = 0) -> dict:
    splits = jax.random.split(jax.random.key(seed), 10)
    right_side = draw_right_side(jax.random.fold_in(splits[9], 71), 0)
    diag_blocks = draw_diag_blocks(jax.random.fold_in(splits[9], 71), 0)
    couplings = scatter_about(splits[2], (NBLK, K, B, B), (4 * B) ** -0.5, 0.25, ((0, 128),), jnp.float32)
    factors = draw_factors(jax.random.fold_in(splits[9], 71), 0)
    prolong = scatter_about(splits[4], (NBLK, NCF, B), (2 * NCF) ** -0.5, 1.5, ((0, 128),), jnp.float32)
    coarse_inverse = draw_coarse_inverse(jax.random.fold_in(splits[9], 71), 0)
    intersection_send = draw_intersection_send(jax.random.fold_in(splits[9], 71), 0)
    neighbours = draw_neighbours(jax.random.fold_in(splits[9], 71), 0)
    coarse_pick = draw_coarse_pick(jax.random.fold_in(splits[9], 71), 0)
    return dict(right_side=right_side, diag_blocks=diag_blocks, couplings=couplings, factors=factors, prolong=prolong, coarse_inverse=coarse_inverse, intersection_send=intersection_send, neighbours=neighbours, coarse_pick=coarse_pick)


HI = lax.Precision.HIGHEST


def ext_blocks(field, intersection_send):
    nrhs = field.shape[1]
    width = field.shape[2]
    grid = field.reshape(N_SUB, N_GRP, BLK_DEV, nrhs, width)
    lists = intersection_send.reshape(N_SUB, N_GRP, HALO)
    sent = jnp.take_along_axis(grid, lists[:, :, :, None, None], axis=2)
    lower = jnp.roll(sent, 1, axis=0)
    upper = jnp.roll(sent, -1, axis=0)
    extended = jnp.concatenate([grid, lower, upper], axis=2)
    return extended.reshape(N_SUB * N_GRP, BLK_DEV + 2 * HALO, nrhs, width)


def apply_operator(field, intersection_send, neighbours, diag_blocks, couplings):
    nrhs = field.shape[1]
    width = field.shape[2]
    extended = ext_blocks(field, intersection_send)
    lists = neighbours.reshape(N_SUB * N_GRP, BLK_DEV, K)
    image = jnp.einsum('nrc,nbc->nrb', field, diag_blocks, precision=HI)
    for slot in range(K):
        picked = jnp.take_along_axis(extended, lists[:, :, slot][:, :, None, None], axis=1)
        picked = picked.reshape(field.shape[0], nrhs, width)
        image = image + jnp.einsum('nrc,nbc->nrb', picked, couplings[:, slot], precision=HI)
    return image


def precondition(residual, factors, prolong, coarse_pick, coarse_inverse):
    nrhs = residual.shape[1]
    per = BLK_DEV // N_SUB
    inner = jnp.einsum('nrb,nbc->nrc', residual, factors, precision=HI)
    fine = jnp.einsum('nrc,nbc->nrb', inner, factors, precision=HI)
    coarse_rhs = jnp.einsum('ncb,nrb->ncr', prolong, residual, precision=HI)
    grid = coarse_rhs.reshape(N_SUB, N_GRP, BLK_DEV, NCF, nrhs)
    picks = coarse_pick.reshape(N_SUB, N_GRP, BLK_DEV)
    slots = jnp.take_along_axis(grid, picks[:, :, :, None, None], axis=2)
    slots = slots.reshape(N_SUB, N_GRP, N_SUB, per, NCF, nrhs)
    vectors = slots.transpose(2, 1, 0, 3, 4, 5).reshape(N_SUB, BLK_DEV * N_GRP * NCF, nrhs)
    solved = jnp.einsum('qij,qjr->qir', coarse_inverse, vectors, precision=HI)
    solved = solved.reshape(N_SUB, N_GRP, N_SUB, per, NCF, nrhs).transpose(2, 1, 0, 3, 4, 5)
    solved = solved.reshape(N_SUB, N_GRP, BLK_DEV, NCF, nrhs)
    inverse = jnp.argsort(picks, axis=-1).astype(jnp.int32)
    coarse_sol = jnp.take_along_axis(solved, inverse[:, :, :, None, None], axis=2)
    coarse_sol = coarse_sol.reshape(residual.shape[0], NCF, nrhs)
    coarse = jnp.einsum('ncb,ncr->nrb', prolong, coarse_sol, precision=HI)
    return fine + coarse


def reference(right_side, diag_blocks, couplings, factors, prolong, coarse_inverse, intersection_send, neighbours, coarse_pick):
    solution = jnp.zeros_like(right_side)
    residual = right_side
    for step in range(ITERS):
        direction = precondition(residual, factors, prolong, coarse_pick, coarse_inverse)
        image = apply_operator(direction, intersection_send, neighbours, diag_blocks, couplings)
        alpha = jnp.sum(image * residual) / jnp.sum(image * image)
        solution = solution + alpha * direction
        residual = residual - alpha * image
    return solution, residual
```

```python
import functools

import jax
import jax.numpy as jnp
from jax import lax
from jax.experimental import pallas as pl
from jax.experimental.pallas import tpu as pltpu
from jax.sharding import PartitionSpec as P

F32 = jnp.float32
BF16 = jnp.bfloat16
TILES = 7
VMEM = 60 * 1024 * 1024
SMALL = 16 * 1024 * 1024


def nn(a, b):
    return lax.dot_general(a, b, (((1,), (0,)), ((), ())), preferred_element_type=F32)


def nt(a, b):
    return lax.dot_general(a, b, (((1,), (1,)), ((), ())), preferred_element_type=F32)


def tn(a, b):
    return lax.dot_general(a, b, (((0,), (0,)), ((), ())), preferred_element_type=F32)


def parts(x):
    head = x.astype(BF16)
    return head, (x - head.astype(F32)).astype(BF16)


def wide(x):
    return jnp.concatenate(parts(x), axis=1)


def fold(x):
    half = x.shape[1] // 2
    return x[:, :half] + x[:, half:]


def weights_nt(w):
    h, l = parts(w)
    return jnp.concatenate([jnp.concatenate([h, h], 1), jnp.concatenate([l, l], 1)], 0)


def weights_nn(w):
    h, l = parts(w)
    row = jnp.concatenate([h, l], 1)
    return jnp.concatenate([row, row], 0)


def rows_by(p):
    return weights_nt(p)


def fold_rows(x):
    half = x.shape[0] // 2
    return x[:half] + x[half:]


def cost(flops, nbytes):
    return pl.CostEstimate(flops=int(flops), bytes_accessed=int(nbytes), transcendentals=0)


SMEM = pl.BlockSpec(memory_space=pltpu.SMEM)
ANY = pl.BlockSpec(memory_space=pl.ANY)
INVMEM = pl.BlockSpec(memory_space=pltpu.VMEM)


def whole(x):
    zeros = (0,) * len(x.shape)
    return pl.BlockSpec(x.shape, lambda *_: zeros)


def lead(x, block, at=lambda i: i):
    tail = (0,) * (len(x.shape) - 1)
    return pl.BlockSpec((block,) + tuple(x.shape[1:]), lambda i, *_: (at(i),) + tail)


def shape_of(shape, kind=F32):
    return jax.ShapeDtypeStruct(shape, kind)


def call(kernel, name, grid, arrays, in_specs, outs, out_specs, flops, scratch=(), limit=VMEM):
    moved = sum(x.nbytes for x in arrays) + sum(x.size * x.dtype.itemsize for x in outs)
    return pl.pallas_call(
        kernel,
        grid=grid,
        in_specs=in_specs,
        out_specs=out_specs,
        out_shape=outs,
        scratch_shapes=list(scratch),
        compiler_params=pltpu.CompilerParams(vmem_limit_bytes=limit),
        cost_estimate=cost(flops, moved),
        name=name,
    )(*arrays)


def each(count, step, body):
    def some(i, _):
        for j in range(step):
            body(i * step + j)
        return 0

    lax.fori_loop(0, count // step, some, 0)


def gathered(ret, cpos, nbr, n):
    tiles = []
    for k in range(5):
        t = cpos[n] if k == 0 else cpos[nbr[n * 4 + k - 1]]
        tiles.append(jnp.concatenate([ret[t], ret[t + 1]], axis=1))
    c = jnp.concatenate(tiles, axis=0)
    h = c.astype(BF16).astype(F32)
    pad = jnp.zeros((8, c.shape[1]), F32)
    return jnp.concatenate([h, c - h, h, pad], axis=0).astype(BF16)


def alpha_of(ret, blocks):
    total = ret[TILES - 1]
    for q in range(1, blocks):
        total = total + ret[q * TILES + TILES - 1]
    return total[0:1, 0:1] / total[1:2, 0:1]


def invert(pick, inv):
    def put(q, _):
        inv[pick[q]] = q
        return 0

    lax.fori_loop(0, pick.shape[0], put, 0)


def first_kernel(pick, r_ref, p_ref, send_ref, inv_ref, *, step):
    i = pl.program_id(0)

    @pl.when(i == 0)
    def _():
        invert(pick, inv_ref)

    for j in range(step):
        rhs = fold_rows(nt(rows_by(p_ref[j]), wide(r_ref[j])))
        slot = inv_ref[i * step + j]
        for g in range(send_ref.shape[0]):
            send_ref[g, slot] = rhs


def first_rhs(pick, r, p, groups):
    nb, nr, b = r.shape
    nc = p.shape[1]
    step = 8
    send = shape_of((groups, nb, nc, nr))
    return call(
        functools.partial(first_kernel, step=step),
        "first_rhs",
        (nb // step,),
        [pick, r, p],
        [SMEM, lead(r, step), lead(p, step)],
        [send, shape_of((nb,), jnp.int32)],
        [whole(send), SMEM],
        2 * 16 * 256 * 256 * nb,
    )


def fine_block(v, f):
    inner = fold(nn(wide(v), weights_nn(f)))
    return fold(nt(wide(inner), weights_nt(f)))


def sent_first_kernel(send, inv, v_ref, f_ref, p_ref, out_ref, v, f, p, sems):
    count = send.shape[0]
    nr = v.shape[1]
    nc = p.shape[1]
    copies = []
    for j in range(count):
        for k, (src, dst) in enumerate(((v_ref, v), (f_ref, f), (p_ref, p))):
            copies.append(pltpu.make_async_copy(src.at[send[j]], dst.at[j], sems.at[k, j]))
    for c in copies:
        c.start()
    for c in copies:
        c.wait()
    for j in range(count):
        out_ref[j, :nr] = fine_block(v[j], f[j])
        out_ref[j, nr : nr + nc] = p[j]
        out_ref[j, nr + nc :] = jnp.full((8, p.shape[2]), inv[send[j]].astype(F32))


def fine_sent(send, inv, v, f, p):
    _, nr, b = v.shape
    nc = p.shape[1]
    count = send.shape[0]
    return call(
        sent_first_kernel,
        "fine_sent",
        (),
        [send, inv, v, f, p],
        [SMEM, SMEM, ANY, ANY, ANY],
        [shape_of((count, nr + nc + 8, b))],
        [INVMEM],
        4 * 256**3 * count,
        [
            pltpu.VMEM((count, nr, b), F32),
            pltpu.VMEM((count, b, b), F32),
            pltpu.VMEM((count, nc, b), F32),
            pltpu.SemaphoreType.DMA((3, count)),
        ],
    )[0]


FINE_STEP = 8
OP_STEP = 4


def fine_operator_kernel(nbr, v_ref, fac_ref, lo_ref, up_ref, d_ref, w_ref, p_ref, *refs, setup, paf):
    refs = list(refs)
    f_ref, af_ref = refs[:2]
    refs = refs[2:]
    paf_ref = refs.pop(0) if paf else None
    if setup:
        g_ref, h_ref = refs[:2]
        refs = refs[2:]
    ext = refs.pop(0)
    kept = refs.pop(0) if paf else None
    if setup:
        pext, grows = refs
    i = pl.program_id(0)
    nb = p_ref.shape[0]
    nr, nc = v_ref.shape[1], p_ref.shape[1]
    halo = lo_ref.shape[0]
    fine_steps = nb // FINE_STEP

    @pl.when(i < fine_steps)
    def _():
        for j in range(FINE_STEP):
            f2 = wide(fine_block(v_ref[j], fac_ref[j]))
            f_ref[j] = f2
            ext[i * FINE_STEP + j] = f2

    @pl.when(i == fine_steps - 1)
    def _():
        for j in range(halo):
            ext[nb + j] = wide(lo_ref[j, :nr])
            ext[nb + halo + j] = wide(up_ref[j, :nr])
        if setup:
            pext[pl.ds(0, nb)] = p_ref[...]
            pext[pl.ds(nb, halo)] = lo_ref[:, nr : nr + nc]
            pext[pl.ds(nb + halo, halo)] = up_ref[:, nr : nr + nc]

    def products(at):
        for j in range(OP_STEP):
            n = at * OP_STEP + j
            p = p_ref[n]
            paf_ref[n] = fold_rows(nt(wide(kept[n]), rows_by(p)).T)
            if setup:
                g = grows[n]
                gh = g.astype(BF16).astype(F32)
                pad = jnp.zeros((8, g.shape[1]), F32)
                g_ref[n] = jnp.concatenate([gh, gh, g - gh, pad], axis=0).astype(BF16)
                thrice = jnp.concatenate([g, g, g, pad], axis=0)
                h = fold_rows(nt(rows_by(p), wide(thrice)))
                hh = h.astype(BF16).astype(F32)
                lane = lax.broadcasted_iota(jnp.int32, h.shape, 1)
                h_ref[n] = jnp.where(lane < 80, hh, h - hh)

    @pl.when(i >= fine_steps)
    def _():
        at = i - fine_steps
        if paf:
            products(jnp.maximum(at - 1, 0))
        for j in range(OP_STEP):
            n = at * OP_STEP + j
            fields = []
            weights = []
            rows = []
            for k in range(5):
                e = n if k == 0 else nbr[n * 4 + k - 1]
                weights.append(weights_nt(d_ref[j] if k == 0 else w_ref[j, k - 1]))
                fields.append(ext[e])
                if setup:
                    p = pext[e]
                    ph = p.astype(BF16).astype(F32)
                    row = [jnp.zeros((nc, 2 * p.shape[1]), F32)] * 5
                    row[k] = jnp.concatenate([ph, p - ph], axis=1)
                    rows.append(jnp.concatenate(row, axis=1))
            lhs = jnp.concatenate(fields, axis=1)
            if setup:
                rows = jnp.concatenate(rows + [jnp.zeros_like(rows[0])], axis=0).astype(BF16)
                lhs = jnp.concatenate([lhs, rows], axis=0)
            got = fold(nt(lhs, jnp.concatenate(weights, axis=1)))
            if setup:
                grows[n] = got[nr : nr + 5 * nc]
                got = got[:nr]
            af_ref[j] = got
            if paf:
                kept[n] = got

    if paf:

        @pl.when(i == pl.num_programs(0) - 1)
        def _():
            products(nb // OP_STEP - 1)


def fine_operator(nbr, v, fac, lo, up, d, w, p, setup=False, paf=True):
    nb, nr, b = v.shape
    nc = p.shape[1]
    fine_steps = nb // FINE_STEP

    def early(i):
        return jnp.minimum(i, fine_steps - 1)

    def late(i):
        return jnp.maximum(i - fine_steps, 0)

    places = nb + 2 * lo.shape[0]
    f2 = shape_of((nb, nr, 2 * b), BF16)
    af = shape_of((nb, nr, b))
    outs = [f2, af]
    out_specs = [lead(f2, FINE_STEP, early), lead(af, OP_STEP, late)]
    scratch = [pltpu.VMEM((places, nr, 2 * b), BF16)]
    if paf:
        more = [shape_of((nb, nc, nr))]
        scratch.append(pltpu.VMEM((nb, nr, b), F32))
        if setup:
            more += [shape_of((nb, b, b), BF16), shape_of((nb, nc, b))]
            scratch += [pltpu.VMEM((places, nc, b), F32), pltpu.VMEM((nb, 5 * nc, b), F32)]
        outs += more
        out_specs += [whole(x) for x in more]
    return call(
        functools.partial(fine_operator_kernel, setup=setup, paf=paf),
        "fine_operator",
        (fine_steps + nb // OP_STEP,),
        [nbr, v, fac, lo, up, d, w, p],
        [
            SMEM,
            lead(v, FINE_STEP, early),
            lead(fac, FINE_STEP, early),
            whole(lo),
            whole(up),
            lead(d, OP_STEP, late),
            lead(w, OP_STEP, late),
            whole(p),
        ],
        outs,
        out_specs,
        14 * 256**3 * nb,
        scratch,
    )


def solve_kernel(v_ref, c_ref, *refs):
    *sums, out_ref, v, res, sems, sem = refs
    steps = v.shape[0]
    copies = [pltpu.make_async_copy(v_ref.at[k], v.at[k], sems.at[k]) for k in range(steps)]
    for c in copies:
        c.start()
    size = v.shape[1]
    sol = None
    for k in range(steps):
        ch, cl = parts(c_ref[0, :, k * size : (k + 1) * size])
        copies[k].wait()
        vh, vl = parts(v[k])
        term = nn(ch, vh) + nn(ch, vl) + nn(cl, vh)
        sol = term if sol is None else sol + term
    ns = res.shape[0]
    half = sol.shape[1] // 2
    total = sums[0][...] + sums[1][...] if sums else jnp.zeros((8, half), F32)
    for s in range(ns):
        rows = sol[8 * s : 8 * s + 8]
        for place, to in ((0, s), (1, (s + 1) % ns), (2, (s - 1) % ns)):
            res[to, 2 * place] = rows[:, :half]
            res[to, 2 * place + 1] = rows[:, half:]
        res[s, TILES - 1] = total
    out = pltpu.make_async_copy(res, out_ref, sem)
    out.start()
    out.wait()


def solve(vec, inverse, ns, sums):
    steps, k, nr = vec.shape
    shape = (ns, TILES, 8, nr // 2)
    return call(
        solve_kernel,
        "coarse_solve",
        (),
        [vec, inverse, *sums],
        [ANY, INVMEM] + [INVMEM] * len(sums),
        [shape_of(shape)],
        [ANY],
        2 * 3 * 256 * k * steps * nr,
        [
            pltpu.VMEM(vec.shape, F32),
            pltpu.VMEM(shape, F32),
            pltpu.SemaphoreType.DMA((steps,)),
            pltpu.SemaphoreType.DMA,
        ],
    )[0]


def next_kernel(cpos, nbr, ret_ref, paf_ref, h_ref, *refs):
    nb = paf_ref.shape[0]
    *old, new_ref, send_ref, slots, sems = refs
    alpha = alpha_of(ret_ref, nb) if old else None

    def one(n):
        c = gathered(ret_ref, cpos, nbr, n)
        rhs = paf_ref[n] + nn(h_ref[n].astype(BF16), c)
        if old:
            rhs = old[0][n] - alpha * rhs
        new_ref[n] = rhs
        slots[lax.div(cpos[n], TILES)] = rhs

    each(nb, 8, one)
    copies = [
        pltpu.make_async_copy(slots, send_ref.at[g], sems.at[g]) for g in range(send_ref.shape[0])
    ]
    for c in copies:
        c.start()
    for c in copies:
        c.wait()


def next_rhs(cpos, nbr, ret, paf, h, groups, old=None):
    nb, nc, nr = paf.shape
    ins = [ret, paf, h] + ([] if old is None else [old])
    return call(
        next_kernel,
        "next_rhs",
        (),
        [cpos, nbr] + ins,
        [SMEM, SMEM] + [INVMEM] * len(ins),
        [shape_of((nb, nc, nr)), shape_of((groups, nb, nc, nr))],
        [INVMEM, ANY],
        2 * 16 * 256 * 128 * nb,
        [pltpu.VMEM((nb, nc, nr), F32), pltpu.SemaphoreType.DMA((groups,))],
    )


def image_kernel(cpos, nbr, *refs, step, later, sent):
    refs = list(refs)
    if sent:
        send = refs.pop(0)
    ret_ref, g_ref, af_ref, r_ref = refs[:4]
    refs = refs[4:]
    old_ref = refs.pop(0) if later else None
    fac_ref = refs.pop(0) if sent else None
    w_ref = refs.pop(0)
    new_r_ref = refs.pop(0) if later else None
    sum_ref = refs.pop(0)
    sent_ref = refs.pop(0) if sent else None
    acc = refs.pop(0)
    if sent:
        kept, fac, sems = refs
    i = pl.program_id(0)
    last = pl.num_programs(0) - 1

    def fetch(j):
        return pltpu.make_async_copy(fac_ref.at[send[j]], fac.at[j], sems.at[j])

    @pl.when(i == 0)
    def _():
        acc[...] = jnp.zeros_like(acc)
        if sent:
            for j in range(fac.shape[0]):
                fetch(j).start()

    if later:
        alpha = alpha_of(ret_ref, cpos.shape[0] - 8)
    upper = acc[0]
    lower = acc[1]
    for j in range(step):
        n = i * step + j
        c = gathered(ret_ref, cpos, nbr, n)
        w = af_ref[j] + tn(c, g_ref[j])
        r = r_ref[j]
        if later:
            old = old_ref[j]
            w = old - alpha * w
            r = r - alpha * old
            new_r_ref[j] = r
        w_ref[j] = w
        if sent:
            kept[n] = w
        upper += jnp.sum((w * r).reshape(-1, 8, w.shape[1]), axis=0)
        lower += jnp.sum((w * w).reshape(-1, 8, w.shape[1]), axis=0)
    acc[0] = upper
    acc[1] = lower

    @pl.when(i == last)
    def _():
        up = jnp.sum(acc[0], keepdims=True)
        low = jnp.sum(acc[1], keepdims=True)
        row = lax.broadcasted_iota(jnp.int32, sum_ref.shape, 0)
        sum_ref[...] = jnp.where(row == 0, up, low)
        if sent:
            for j in range(fac.shape[0]):
                fetch(j).wait()
            for j in range(fac.shape[0]):
                sent_ref[j] = fine_block(kept[send[j]], fac[j])


def image_of(cpos, nbr, ret, g, af, r, old=None, send=None, fac=None):
    nb, nr, b = af.shape
    step = 4
    later = old is not None
    sent = send is not None
    big = lead(af, step)
    ins = [cpos, nbr]
    specs = [SMEM, SMEM]
    if sent:
        ins.append(send)
        specs.append(SMEM)
    ins += [ret, g, af, r]
    specs += [whole(ret), lead(g, step), big, big]
    if later:
        ins.append(old)
        specs.append(big)
    outs = [af] * (2 if later else 1)
    out_specs = [big] * len(outs)
    sums = shape_of((8, b))
    outs.append(sums)
    out_specs.append(whole(sums))
    scratch = [pltpu.VMEM((2, 8, b), F32)]
    if sent:
        ins.append(fac)
        specs.append(ANY)
        count = send.shape[0]
        sent_blocks = shape_of((count, nr, b))
        outs.append(sent_blocks)
        out_specs.append(whole(sent_blocks))
        scratch += [
            pltpu.VMEM((nb, nr, b), F32),
            pltpu.VMEM((count, b, b), F32),
            pltpu.SemaphoreType.DMA((count,)),
        ]
    return call(
        functools.partial(image_kernel, step=step, later=later, sent=sent),
        "image",
        (nb // step,),
        ins,
        specs,
        [shape_of(x.shape) for x in outs],
        out_specs,
        2 * 256 * 128 * 128 * nb,
        scratch,
    )


def combine_kernel(cpos, r0_ref, r1_ref, r2_ref, p_ref, f0_ref, f1_ref, f2_ref, s_ref, d_ref, *, step):
    i = pl.program_id(0)
    nb = cpos.shape[0] - 8
    a0 = alpha_of(r1_ref, nb)
    a1 = alpha_of(r2_ref, nb)
    for j in range(step):
        p = p_ref[j]
        ph = p.astype(BF16).astype(F32)
        p3 = jnp.concatenate([ph, ph, p - ph, jnp.zeros_like(p)], axis=0).astype(BF16)
        t = cpos[i * step + j]
        found = []
        for ret, f_ref in ((r0_ref, f0_ref), (r1_ref, f1_ref), (r2_ref, f2_ref)):
            c = jnp.concatenate([ret[t], ret[t + 1]], axis=1)
            h = c.astype(BF16).astype(F32)
            c3 = jnp.concatenate([h, c - h, h, jnp.zeros_like(h)], axis=0).astype(BF16)
            fine = f_ref[j].astype(F32)
            found.append(fold(fine) + tn(c3, p3))
        d0 = found[0]
        d1 = d0 - a0 * found[1]
        s_ref[j] = a0 * d0 + a1 * d1
        d_ref[j] = d1 - a1 * found[2]


def combine(cpos, rets, p, fs):
    nb, _, b = p.shape
    nr = fs[0].shape[1]
    step = 4
    out = shape_of((nb, nr, b))
    return call(
        functools.partial(combine_kernel, step=step),
        "combine",
        (nb // step,),
        [cpos, *rets, p, *fs],
        [SMEM] + [whole(x) for x in rets] + [lead(p, step)] + [lead(f, step) for f in fs],
        [out, out],
        [lead(out, step)] * 2,
        2 * 3 * 256 * 128 * 128 * nb,
    )


def shifted(x, axis, by):
    count = lax.axis_size(axis)
    return lax.ppermute(x, axis, [(i, (i + by) % count) for i in range(count)])


def both_ways(x):
    return shifted(x, "sub", 1), shifted(x, "sub", -1)


def local(
    right_side,
    diag_blocks,
    couplings,
    factors,
    prolong,
    coarse_inverse,
    intersection_send,
    neighbours,
    coarse_pick,
):
    nb, nr, b = right_side.shape
    nc = prolong.shape[1]
    ns = lax.axis_size("sub")
    ng = lax.axis_size("grp")
    nbr = neighbours.reshape(-1)

    def exchange(send):
        flat = send.reshape(ng * nb, nc, nr)
        got = lax.all_to_all(flat, ("grp", "sub"), split_axis=0, concat_axis=0, tiled=True)
        return got.reshape(ng, nb * nc, nr)

    def coarse(vec, sums):
        out = solve(vec, coarse_inverse, ns, sums)
        back = lax.all_to_all(out, "sub", split_axis=0, concat_axis=0, tiled=True)
        return back.reshape(ns * TILES, 8, nr // 2)

    def over_grp(sums):
        sums = sums + lax.ppermute(sums, "grp", [(i, i ^ 1) for i in range(ng)])
        return sums, lax.ppermute(sums, "grp", [(i, ng - 1 - i) for i in range(ng)])

    def places(x):
        return x[:, nr + nc, 0].astype(jnp.int32) * TILES

    weights = (diag_blocks, couplings, prolong)
    send, inv = first_rhs(coarse_pick, right_side, prolong, ng)
    vec0 = exchange(send)
    lo, up = both_ways(fine_sent(intersection_send, inv, right_side, factors, prolong))
    cpos = jnp.concatenate([inv * TILES, places(lo) + 2, places(up) + 4])
    f0, af0, paf0, g, h = fine_operator(nbr, right_side, factors, lo, up, *weights, setup=True)
    ret0 = coarse(vec0, ())

    pw0, send = next_rhs(cpos, nbr, ret0, paf0, h, ng)
    vec1 = exchange(send)
    w0, sums, sent = image_of(
        cpos, nbr, ret0, g, af0, right_side, None, intersection_send, factors
    )
    lo, up = both_ways(sent)
    sums = over_grp(sums)
    f1, af1, paf1 = fine_operator(nbr, w0, factors, lo, up, *weights)
    ret1 = coarse(vec1, sums)

    _, send = next_rhs(cpos, nbr, ret1, paf1, h, ng, pw0)
    vec2 = exchange(send)
    w1, r1, sums, sent = image_of(
        cpos, nbr, ret1, g, af1, right_side, w0, intersection_send, factors
    )
    lo, up = both_ways(sent)
    sums = over_grp(sums)
    f2, af2 = fine_operator(nbr, w1, factors, lo, up, *weights, paf=False)
    ret2 = coarse(vec2, sums)

    w2, r2, sums = image_of(cpos, nbr, ret2, g, af2, r1, w1)
    every = jnp.broadcast_to(sums[None, :1], (ns * ng, 1, b))
    every = jnp.concatenate([every, jnp.broadcast_to(sums[None, 1:2], (ns * ng, 1, b))], axis=1)
    every = lax.all_to_all(every, ("grp", "sub"), split_axis=0, concat_axis=0, tiled=True)
    s2, d2 = combine(cpos, (ret0, ret1, ret2), prolong, (f0, f1, f2))
    total = jnp.sum(every[:, :, 0], axis=0)
    alpha = total[0] / total[1]
    return s2 + alpha * d2, r2 - alpha * w2


def solution(mesh):
    return jax.shard_map(
        local,
        mesh=mesh,
        in_specs=(
            P(("sub", "grp"), None, None),
            P(("sub", "grp"), None, None),
            P(("sub", "grp"), None, None, None),
            P(("sub", "grp"), None, None),
            P(("sub", "grp"), None, None),
            P("sub", "grp", None),
            P(("sub", "grp")),
            P(("sub", "grp"), None),
            P(("sub", "grp")),
        ),
        out_specs=(P(("sub", "grp"), None, None), P(("sub", "grp"), None, None)),
        check_vma=False,
    )
```

```python
import functools

import jax
import jax.numpy as jnp
from jax import lax
from jax.experimental import pallas as pl
from jax.experimental.pallas import tpu as pltpu
from jax.sharding import PartitionSpec as P

F32 = jnp.float32
BF16 = jnp.bfloat16
TILES = 6
MIB = 1024 * 1024
CHUNK = 8


def nn(a, b):
    return lax.dot_general(a, b, (((1,), (0,)), ((), ())), preferred_element_type=F32)


def nt(a, b):
    return lax.dot_general(a, b, (((1,), (1,)), ((), ())), preferred_element_type=F32)


def tn(a, b):
    return lax.dot_general(a, b, (((0,), (0,)), ((), ())), preferred_element_type=F32)


def parts(x):
    head = x.astype(BF16)
    return head, (x - head.astype(F32)).astype(BF16)


def wide(x):
    return jnp.concatenate(parts(x), axis=1)


def fold(x):
    half = x.shape[1] // 2
    return x[:, :half] + x[:, half:]


def weights_nt(w):
    h, l = parts(w)
    return jnp.concatenate([jnp.concatenate([h, h], 1), jnp.concatenate([l, l], 1)], 0)


def weights_nn(w):
    h, l = parts(w)
    row = jnp.concatenate([h, l], 1)
    return jnp.concatenate([row, row], 0)


def rows_by(p):
    return weights_nt(p)


def fold_rows(x):
    half = x.shape[0] // 2
    return x[:half] + x[half:]


def cost(flops, nbytes):
    return pl.CostEstimate(flops=int(flops), bytes_accessed=int(nbytes), transcendentals=0)


SMEM = pl.BlockSpec(memory_space=pltpu.SMEM)
HBM = pl.BlockSpec(memory_space=pltpu.HBM)
INVMEM = pl.BlockSpec(memory_space=pltpu.VMEM)


def shape_of(shape, kind=F32):
    return jax.ShapeDtypeStruct(shape, kind)


def call(kernel, name, arrays, in_specs, outs, out_specs, flops, scratch=(), limit=58):
    moved = sum(x.nbytes for x in arrays) + sum(x.size * x.dtype.itemsize for x in outs)
    return pl.pallas_call(
        kernel,
        in_specs=in_specs,
        out_specs=out_specs,
        out_shape=outs,
        scratch_shapes=list(scratch),
        compiler_params=pltpu.CompilerParams(vmem_limit_bytes=limit * MIB),
        cost_estimate=cost(flops, moved),
        name=name,
    )(*arrays)


def chunk(src, dst, sems, i):
    at = pl.ds(i * CHUNK, CHUNK)
    return pltpu.make_async_copy(src.at[at], dst.at[at], sems.at[i])


def loop(count, body):
    def one(i, _):
        body(i)
        return 0

    lax.fori_loop(0, count, one, 0)


def stacked(c):
    h = c.astype(BF16).astype(F32)
    pad = jnp.zeros((-3 * c.shape[0] % 16, c.shape[1]), F32)
    return jnp.concatenate([h, c - h, h, pad], axis=0).astype(BF16)


def correction(ret, width, t):
    at = lax.div(t, TILES) * width + lax.rem(t, TILES)
    return jnp.concatenate([ret[at], ret[at + 1]], axis=1)


def gathered(find, cpos, nbr, n):
    tiles = []
    for k in range(5):
        tiles.append(find(cpos[n] if k == 0 else cpos[nbr[n * 4 + k - 1]]))
    return stacked(jnp.concatenate(tiles, axis=0))


def alpha_of(planes):
    total = planes[0][...]
    for x in planes[1:]:
        total = total + x[...]
    return total[0:1, 0:1] / total[1:2, 0:1]


def invert(pick, inv):
    def put(q, _):
        inv[pick[q]] = q
        return 0

    lax.fori_loop(0, pick.shape[0], put, 0)


def first_kernel(pick, r_ref, p_ref, send_ref, inv_ref, r, slots, sems, out_sems):
    nb = r.shape[0]
    for i in range(nb // CHUNK):
        chunk(r_ref, r, sems, i).start()
    invert(pick, inv_ref)

    def some(i):
        chunk(r_ref, r, sems, i).wait()
        for j in range(CHUNK):
            n = i * CHUNK + j
            slots[inv_ref[n]] = fold_rows(nt(rows_by(p_ref[n]), wide(r[n])))

    loop(nb // CHUNK, some)
    copies = [
        pltpu.make_async_copy(slots, send_ref.at[g], out_sems.at[g])
        for g in range(send_ref.shape[0])
    ]
    for c in copies:
        c.start()
    for c in copies:
        c.wait()


def first_rhs(pick, r, p, groups):
    nb, nr, b = r.shape
    nc = p.shape[1]
    return call(
        first_kernel,
        "first_rhs",
        [pick, r, p],
        [SMEM, HBM, INVMEM],
        [shape_of((groups, nb, nc, nr)), shape_of((nb,), jnp.int32)],
        [HBM, SMEM],
        2 * 16 * 256 * 256 * nb,
        [
            pltpu.VMEM(r.shape, F32),
            pltpu.VMEM((nb, nc, nr), F32),
            pltpu.SemaphoreType.DMA((nb // CHUNK,)),
            pltpu.SemaphoreType.DMA((groups,)),
        ],
    )


def fine_block(v, f):
    inner = fold(nn(wide(v), weights_nn(f)))
    return fold(nt(wide(inner), weights_nt(f)))


def fine_first_kernel(send, inv, v_hbm, fac_hbm, p_ref, f_hbm, out_ref, v, fac, ext, v_sem, fac_sem, f_sem):
    steps = v.shape[0] // CHUNK
    nr = v.shape[1]
    nc = p_ref.shape[1]
    for i in range(steps):
        chunk(v_hbm, v, v_sem, i).start()
        chunk(fac_hbm, fac, fac_sem, i).start()

    def some(i):
        chunk(v_hbm, v, v_sem, i).wait()
        chunk(fac_hbm, fac, fac_sem, i).wait()
        for j in range(CHUNK):
            n = i * CHUNK + j
            ext[n] = wide(fine_block(v[n], fac[n]))
        chunk(ext, f_hbm, f_sem, i).start()

    loop(steps, some)
    for j in range(send.shape[0]):
        n = send[j]
        out_ref[j, :nr] = fold(ext[n].astype(F32))
        out_ref[j, nr : nr + nc] = p_ref[n]
        out_ref[j, nr + nc :] = jnp.full((8, p_ref.shape[2]), inv[n].astype(F32))
    for i in range(steps):
        chunk(ext, f_hbm, f_sem, i).wait()


def fine_first(send, inv, v, fac, p):
    nb, nr, b = v.shape
    nc = p.shape[1]
    return call(
        fine_first_kernel,
        "fine_first",
        [send, inv, v, fac, p],
        [SMEM, SMEM, HBM, HBM, INVMEM],
        [shape_of((nb, nr, 2 * b), BF16), shape_of((send.shape[0], nr + nc + 8, b))],
        [HBM, INVMEM],
        4 * 256**3 * nb,
        [
            pltpu.VMEM(v.shape, F32),
            pltpu.VMEM(fac.shape, F32),
            pltpu.VMEM((nb, nr, 2 * b), BF16),
        ]
        + [pltpu.SemaphoreType.DMA((nb // CHUNK,))] * 3,
    )


def operator_kernel(nbr, f_hbm, lo_ref, up_ref, d_hbm, w_hbm, p_ref, *refs, setup, paf):
    refs = list(refs)
    af_hbm = refs.pop(0)
    paf_ref = refs.pop(0) if paf else None
    if setup:
        g_ref, h_ref, pext, grows = refs[:2] + refs[-2:]
        refs = refs[2:-2]
    d, w, ext, kept, d_sem, w_sem, f_sem, af_sem = refs
    nb, nr, b = kept.shape
    nc = p_ref.shape[1]
    halo = lo_ref.shape[0]
    steps = nb // CHUNK

    for i in range(steps):
        chunk(f_hbm, ext, f_sem, i).start()
    for i in range(steps):
        chunk(d_hbm, d, d_sem, i).start()
        chunk(w_hbm, w, w_sem, i).start()
    for j in range(halo):
        ext[nb + j] = wide(lo_ref[j, :nr])
        ext[nb + halo + j] = wide(up_ref[j, :nr])
    if setup:
        pext[pl.ds(0, nb)] = p_ref[...]
        pext[pl.ds(nb, halo)] = lo_ref[:, nr : nr + nc]
        pext[pl.ds(nb + halo, halo)] = up_ref[:, nr : nr + nc]
    for i in range(steps):
        chunk(f_hbm, ext, f_sem, i).wait()

    def products(i):
        for j in range(CHUNK):
            n = i * CHUNK + j
            p = p_ref[n]
            paf_ref[n] = fold_rows(nt(wide(kept[n]), rows_by(p)).T)
            if setup:
                g = grows[n]
                gh = g.astype(BF16).astype(F32)
                pad = jnp.zeros((8, g.shape[1]), F32)
                g_ref[n] = jnp.concatenate([gh, gh, g - gh, pad], axis=0).astype(BF16)
                thrice = jnp.concatenate([g, g, g, pad], axis=0)
                h = fold_rows(nt(rows_by(p), wide(thrice)))
                hh = h.astype(BF16).astype(F32)
                lane = lax.broadcasted_iota(jnp.int32, h.shape, 1)
                h_ref[n] = jnp.where(lane < 80, hh, h - hh)

    def image(i):
        chunk(d_hbm, d, d_sem, i).wait()
        chunk(w_hbm, w, w_sem, i).wait()
        if paf and i:
            products(i - 1)
        for j in range(CHUNK):
            n = i * CHUNK + j
            fields = []
            weights = []
            rows = []
            for k in range(5):
                e = n if k == 0 else nbr[n * 4 + k - 1]
                weights.append(weights_nt(d[n] if k == 0 else w[n, k - 1]))
                fields.append(ext[e])
                if setup:
                    p = pext[e]
                    ph = p.astype(BF16).astype(F32)
                    row = [jnp.zeros((nc, 2 * b), F32)] * 5
                    row[k] = jnp.concatenate([ph, p - ph], axis=1)
                    rows.append(jnp.concatenate(row, axis=1))
            lhs = jnp.concatenate(fields, axis=1)
            if setup:
                rows = jnp.concatenate(rows + [jnp.zeros_like(rows[0])], axis=0).astype(BF16)
                lhs = jnp.concatenate([lhs, rows], axis=0)
            got = fold(nt(lhs, jnp.concatenate(weights, axis=1)))
            if setup:
                grows[n] = got[nr : nr + 5 * nc]
                got = got[:nr]
            kept[n] = got
        chunk(kept, af_hbm, af_sem, i).start()

    for i in range(steps):
        image(i)
    if paf:
        products(steps - 1)
    for i in range(steps):
        chunk(kept, af_hbm, af_sem, i).wait()


def operator(nbr, f, lo, up, d, w, p, setup=False, paf=True):
    nb, nc, b = p.shape
    nr = f.shape[1]
    places = nb + 2 * lo.shape[0]
    outs = [shape_of((nb, nr, b))]
    scratch = [pltpu.VMEM(d.shape, F32), pltpu.VMEM(w.shape, F32)]
    scratch += [pltpu.VMEM((places, nr, 2 * b), BF16), pltpu.VMEM((nb, nr, b), F32)]
    scratch += [pltpu.SemaphoreType.DMA((nb // CHUNK,))] * 4
    if paf:
        outs.append(shape_of((nb, nc, nr)))
    if setup:
        outs += [shape_of((nb, b, b), BF16), shape_of((nb, nc, b))]
        scratch += [pltpu.VMEM((places, nc, b), F32), pltpu.VMEM((nb, 5 * nc, b), F32)]
    return call(
        functools.partial(operator_kernel, setup=setup, paf=paf),
        "operator",
        [nbr, f, lo, up, d, w, p],
        [SMEM, HBM, INVMEM, INVMEM, HBM, HBM, INVMEM],
        outs,
        [HBM] + [INVMEM] * (len(outs) - 1),
        10 * 256**3 * nb,
        scratch,
    )


def solve_kernel(v_ref, c_ref, *refs):
    *sums, out_ref, res, sem = refs
    vh, vl = parts(v_ref[...])
    ch, cl = parts(c_ref[0])
    sol = nn(ch, vh) + nn(ch, vl) + nn(cl, vh)
    ns = res.shape[0]
    half = sol.shape[1] // 2
    for s in range(ns):
        rows = sol[8 * s : 8 * s + 8]
        for place, to in ((0, s), (1, (s + 1) % ns), (2, (s - 1) % ns)):
            res[to, 2 * place] = rows[:, :half]
            res[to, 2 * place + 1] = rows[:, half:]
        if sums:
            res[s, TILES] = sums[0][...]
    out = pltpu.make_async_copy(res, out_ref, sem)
    out.start()
    out.wait()


def solve(vec, inverse, ns, sums):
    k, nr = vec.shape
    shape = (ns, TILES + len(sums), 8, nr // 2)
    return call(
        solve_kernel,
        "coarse_solve",
        [vec, inverse, *sums],
        [INVMEM, INVMEM] + [INVMEM] * len(sums),
        [shape_of(shape)],
        [HBM],
        2 * 3 * 256 * k * nr,
        [pltpu.VMEM(shape, F32), pltpu.SemaphoreType.DMA],
        24,
    )[0]


def next_kernel(pick, cpos, nbr, ret_ref, paf_ref, h_ref, *refs, width):
    nb = paf_ref.shape[0]
    send_ref, slots, sems = refs
    groups = send_ref.shape[0]

    def out(i, g):
        at = pl.ds(i * CHUNK, CHUNK)
        return pltpu.make_async_copy(slots.at[at], send_ref.at[g, at], sems.at[g, i])

    def some(i):
        for j in range(CHUNK):
            q = i * CHUNK + j
            n = pick[q]
            c = gathered(lambda t: correction(ret_ref, width, t), cpos, nbr, n)
            slots[q] = paf_ref[n] + nn(h_ref[n].astype(BF16), c)
        for g in range(groups):
            out(i, g).start()

    loop(nb // CHUNK, some)
    for i in range(nb // CHUNK):
        for g in range(groups):
            out(i, g).wait()


def next_rhs(pick, cpos, nbr, ret, width, paf, h, groups):
    nb, nc, nr = paf.shape
    return call(
        functools.partial(next_kernel, width=width),
        "next_rhs",
        [pick, cpos, nbr, ret, paf, h],
        [SMEM] * 3 + [INVMEM] * 3,
        [shape_of((groups, nb, nc, nr))],
        [HBM],
        2 * 16 * 256 * 128 * nb,
        [pltpu.VMEM((nb, nc, nr), F32), pltpu.SemaphoreType.DMA((groups, nb // CHUNK))],
        24,
    )


def image_kernel(cpos, nbr, *refs, stage, widths):
    refs = list(refs)

    def take(count):
        found = refs[:count]
        del refs[:count]
        return found

    send = None if stage == 2 else refs.pop(0)
    planes = take(4) if stage else []
    rets = take(2 if stage == 2 else 1)
    g_hbm, af_hbm, r_hbm = take(3)
    old_hbm = refs.pop(0) if stage else None
    fac_hbm = None if stage == 2 else refs.pop(0)
    before_ref = refs.pop(0) if stage == 2 else None
    w_out = refs.pop(0)
    r_out = refs.pop(0) if stage == 1 else None
    f_out = None if stage == 2 else refs.pop(0)
    sum_ref = refs.pop(0)
    sent_ref = None if stage == 2 else refs.pop(0)
    af, r, g, af_sem, r_sem, g_sem, w_sem = take(7)
    if stage:
        old, old_sem = take(2)
    if stage < 2:
        fac, ext, fac_sem, r_out_sem, f_sem = take(5)
    nb = af.shape[0]
    steps = nb // CHUNK

    def ins(i):
        found = [chunk(af_hbm, af, af_sem, i), chunk(r_hbm, r, r_sem, i), chunk(g_hbm, g, g_sem, i)]
        if stage:
            found.append(chunk(old_hbm, old, old_sem, i))
        if stage < 2:
            found.append(chunk(fac_hbm, fac, fac_sem, i))
        return found

    def outs(i):
        found = [chunk(af, w_out, w_sem, i)]
        if stage == 1:
            found.append(chunk(r, r_out, r_out_sem, i))
        return found

    for i in range(steps):
        for c in ins(i):
            c.start()
    alpha = alpha_of(planes) if stage else None

    def find(t):
        c = correction(rets[0], widths[0], t)
        if stage == 2:
            c = c - alpha * correction(rets[1], widths[1], t)
        return c

    def fine(i):
        for j in range(CHUNK):
            n = i * CHUNK + j
            ext[n] = wide(fine_block(af[n], fac[n]))
        chunk(ext, f_out, f_sem, i).start()

    def some(i, acc):
        acc = list(acc)
        for c in ins(i):
            c.wait()
        for j in range(CHUNK):
            n = i * CHUNK + j
            w = af[n] + tn(gathered(find, cpos, nbr, n), g[n])
            res = r[n]
            if stage == 0:
                pairs = ((w, res), (w, w))
            elif stage == 1:
                before = old[n]
                w = before - alpha * w
                res = res - alpha * before
                r[n] = res
                pairs = ((w, res), (w, w))
            else:
                pairs = ((w, res), (w, w), (w, old[n]))
            af[n] = w
            for k, (x, y) in enumerate(pairs):
                acc[k] += jnp.sum((x * y).reshape(-1, 8, w.shape[1]), axis=0)
        if stage < 2 and i:
            fine(i - 1)
        for c in outs(i):
            c.start()
        return acc

    zero = jnp.zeros((8, af.shape[2]), F32)
    acc = [zero] * (3 if stage == 2 else 2)
    for i in range(steps):
        acc = some(i, acc)
    acc = [jnp.sum(x, keepdims=True) for x in acc]
    shape = (2, af.shape[2]) if stage == 2 else sum_ref.shape
    row = lax.broadcasted_iota(jnp.int32, shape, 1 if stage == 2 else 0)
    if stage == 2:
        acc += [before_ref[0:1, 0:1], before_ref[1:2, 0:1]]
    total = jnp.zeros(shape, F32)
    for k, x in enumerate(acc):
        total = jnp.where(row == k, x, total)
    if stage == 2:
        for k in range(sum_ref.shape[0]):
            sum_ref[k] = total
    else:
        sum_ref[...] = total
        fine(steps - 1)
        for j in range(send.shape[0]):
            sent_ref[j] = fold(ext[send[j]].astype(F32))
        for i in range(steps):
            chunk(ext, f_out, f_sem, i).wait()
    for i in range(steps):
        for c in outs(i):
            c.wait()


def image_of(stage, cpos, nbr, rets, widths, g, af, r, planes=(), old=None, send=None, fac=None, before=None, everyone=0):
    nb, nr, b = af.shape
    steps = nb // CHUNK
    dma = pltpu.SemaphoreType.DMA
    ins = [cpos, nbr] + ([] if send is None else [send])
    specs = [SMEM] * len(ins)
    ins += [*planes, *rets, g, af, r]
    specs += [INVMEM] * (len(planes) + len(rets)) + [HBM] * 3
    scratch = [pltpu.VMEM(af.shape, F32), pltpu.VMEM(af.shape, F32), pltpu.VMEM(g.shape, BF16)]
    scratch += [dma((steps,))] * 4
    if stage:
        ins.append(old)
        specs.append(HBM)
        scratch += [pltpu.VMEM(af.shape, F32), dma((steps,))]
    outs = [shape_of(af.shape)] * (2 if stage == 1 else 1)
    if stage < 2:
        outs.append(shape_of((nb, nr, 2 * b), BF16))
    out_specs = [HBM] * len(outs)
    if stage < 2:
        count = send.shape[0]
        ins.append(fac)
        specs.append(HBM)
        outs += [shape_of((8, b)), shape_of((count, nr, b))]
        scratch += [pltpu.VMEM(fac.shape, F32), pltpu.VMEM((nb, nr, 2 * b), BF16)]
        scratch += [dma((steps,))] * 3
    else:
        ins.append(before)
        specs.append(INVMEM)
        outs.append(shape_of((everyone, 2, b)))
    out_specs += [INVMEM] * (len(outs) - len(out_specs))
    return call(
        functools.partial(image_kernel, stage=stage, widths=widths),
        "image",
        ins,
        specs,
        outs,
        out_specs,
        2 * 256 * 128 * 128 * nb,
        scratch,
        58,
    )


def final_kernel(cpos, *refs, widths):
    planes, sum_ref, rets, p_ref = refs[:4], refs[4], refs[5:8], refs[8]
    hbms, (s_hbm, r_hbm) = refs[9:15], refs[15:17]
    s, res, *refs = refs[17:]
    bufs, (s_sem, r_sem), sems = refs[:6], refs[6:8], refs[8:]
    nb = p_ref.shape[0]
    for i in range(nb // CHUNK):
        for k in range(6):
            chunk(hbms[k], bufs[k], sems[k], i).start()
    fs, (w, r, y) = bufs[:3], bufs[3:]
    total = jnp.sum(sum_ref[...], axis=0)
    yr, yy, yw, wr, ww = (total[0:1, k : k + 1] for k in range(5))
    a0 = alpha_of(planes)
    a1 = wr / ww
    a2 = (wr - a1 * ww - a1 * yr + a1 * a1 * yw) / (ww - 2.0 * a1 * yw + a1 * a1 * yy)
    b0 = a0 + a1 + a2
    b1 = -a0 * (a1 + a2)
    b2 = -a1 * a2

    def some(i):
        for k in range(6):
            chunk(hbms[k], bufs[k], sems[k], i).wait()
        for j in range(CHUNK):
            n = i * CHUNK + j
            p = p_ref[n]
            ph = p.astype(BF16).astype(F32)
            p3 = jnp.concatenate([ph, ph, p - ph, jnp.zeros_like(p)], axis=0).astype(BF16)
            c0, c1, cy = (correction(x, k, cpos[n]) for x, k in zip(rets, widths))
            c = b0 * c0 + (b1 + b2) * c1 - b2 * a0 * cy
            f0, f1, f2 = (fold(x[n].astype(F32)) for x in fs)
            s[n] = b0 * f0 + b1 * f1 + b2 * f2 + tn(stacked(c), p3)
            res[n] = r[n] - (a1 + a2) * w[n] + a1 * a2 * y[n]
        chunk(s, s_hbm, s_sem, i).start()
        chunk(res, r_hbm, r_sem, i).start()

    loop(nb // CHUNK, some)
    for i in range(nb // CHUNK):
        chunk(s, s_hbm, s_sem, i).wait()
        chunk(res, r_hbm, r_sem, i).wait()


def final(cpos, planes, sums, rets, widths, p, fs, w, r, y):
    nb = p.shape[0]
    return call(
        functools.partial(final_kernel, widths=widths),
        "final",
        [cpos, *planes, sums, *rets, p, *fs, w, r, y],
        [SMEM] + [INVMEM] * 9 + [HBM] * 6,
        [shape_of(w.shape)] * 2,
        [HBM, HBM],
        2 * 256 * 128 * 128 * nb,
        [pltpu.VMEM(w.shape, F32)] * 2
        + [pltpu.VMEM(x.shape, x.dtype) for x in (*fs, w, r, y)]
        + [pltpu.SemaphoreType.DMA((nb // CHUNK,))] * 8,
        56,
    )


def shifted(x, axis, by):
    count = lax.axis_size(axis)
    return lax.ppermute(x, axis, [(i, (i + by) % count) for i in range(count)])


def both_ways(x):
    return shifted(x, "sub", 1), shifted(x, "sub", -1)


def local(
    right_side,
    diag_blocks,
    couplings,
    factors,
    prolong,
    coarse_inverse,
    intersection_send,
    neighbours,
    coarse_pick,
):
    nb, nr, b = right_side.shape
    nc = prolong.shape[1]
    ns = lax.axis_size("sub")
    ng = lax.axis_size("grp")
    nbr = neighbours.reshape(-1)

    def exchange(send):
        flat = send.reshape(ng * nb, nc, nr)
        got = lax.all_to_all(flat, ("grp", "sub"), split_axis=0, concat_axis=0, tiled=True)
        return got.reshape(ng * nb * nc, nr)

    def coarse(vec, *sums):
        out = solve(vec, coarse_inverse, ns, sums)
        back = lax.all_to_all(out, "sub", split_axis=0, concat_axis=0, tiled=True)
        return back.reshape(-1, 8, nr // 2)

    def places(x):
        return x[:, nr + nc, 0].astype(jnp.int32) * TILES

    weights = (diag_blocks, couplings, prolong)
    widths = (TILES, TILES + 1, TILES)
    send, inv = first_rhs(coarse_pick, right_side, prolong, ng)
    vec0 = exchange(send)
    f0, sent = fine_first(intersection_send, inv, right_side, factors, prolong)
    lo, up = both_ways(sent)
    cpos = jnp.concatenate([inv * TILES, places(lo) + 2, places(up) + 4])
    af0, paf0, g, h = operator(nbr, f0, lo, up, *weights, setup=True)
    ret0 = coarse(vec0)

    (send,) = next_rhs(coarse_pick, cpos, nbr, ret0, widths[0], paf0, h, ng)
    vec1 = exchange(send)
    w0, f1, sums0, sent = image_of(
        0, cpos, nbr, [ret0], widths[:1], g, af0, right_side, send=intersection_send, fac=factors
    )
    lo, up = both_ways(sent)
    af1, paf1 = operator(nbr, f1, lo, up, *weights)
    ret1 = coarse(vec1, sums0)

    plane = jnp.sum(ret1.reshape(ns, TILES + 1, 8, nr // 2)[:, TILES], axis=0)
    (send,) = next_rhs(coarse_pick, cpos, nbr, ret1, widths[1], paf1, h, ng)
    planes = [plane] + [shifted(plane, "grp", k) for k in range(1, ng)]
    vec2 = exchange(send)
    w1, r1, f2, sums1, sent = image_of(
        1, cpos, nbr, [ret1], widths[1:2], g, af1, right_side, planes, w0, intersection_send, factors
    )
    lo, up = both_ways(sent)
    (af2,) = operator(nbr, f2, lo, up, *weights, paf=False)
    ret2 = coarse(vec2)

    y1, sums = image_of(
        2, cpos, nbr, [ret1, ret2], widths[1:], g, af2, r1, planes, w1, before=sums1, everyone=ns * ng
    )
    sums = lax.all_to_all(sums, ("grp", "sub"), split_axis=0, concat_axis=0, tiled=True)
    return final(cpos, planes, sums, (ret0, ret1, ret2), widths, prolong, (f0, f1, f2), w1, r1, y1)


def solution(mesh):
    return jax.shard_map(
        local,
        mesh=mesh,
        in_specs=(
            P(("sub", "grp"), None, None),
            P(("sub", "grp"), None, None),
            P(("sub", "grp"), None, None, None),
            P(("sub", "grp"), None, None),
            P(("sub", "grp"), None, None),
            P("sub", "grp", None),
            P(("sub", "grp")),
            P(("sub", "grp"), None),
            P(("sub", "grp")),
        ),
        out_specs=(P(("sub", "grp"), None, None), P(("sub", "grp"), None, None)),
        check_vma=False,
    )
```

```python
import functools

import jax
import jax.numpy as jnp
from jax import lax
from jax.experimental import pallas as pl
from jax.experimental.pallas import tpu as pltpu
from jax.sharding import PartitionSpec as P

F32 = jnp.float32
BF16 = jnp.bfloat16
TILES = 6
MIB = 1024 * 1024
CHUNK = 8


def nn(a, b):
    return lax.dot_general(a, b, (((1,), (0,)), ((), ())), preferred_element_type=F32)


def nt(a, b):
    return lax.dot_general(a, b, (((1,), (1,)), ((), ())), preferred_element_type=F32)


def tn(a, b):
    return lax.dot_general(a, b, (((0,), (0,)), ((), ())), preferred_element_type=F32)


def parts(x):
    head = x.astype(BF16)
    return head, (x - head.astype(F32)).astype(BF16)


def wide(x):
    return jnp.concatenate(parts(x), axis=1)


def fold(x):
    half = x.shape[1] // 2
    return x[:, :half] + x[:, half:]


def weights_nt(w):
    h, l = parts(w)
    return jnp.concatenate([jnp.concatenate([h, h], 1), jnp.concatenate([l, l], 1)], 0)


def weights_nn(w):
    h, l = parts(w)
    row = jnp.concatenate([h, l], 1)
    return jnp.concatenate([row, row], 0)


def rows_by(p):
    return weights_nt(p)


def fold_rows(x):
    half = x.shape[0] // 2
    return x[:half] + x[half:]


def cost(flops, nbytes):
    return pl.CostEstimate(flops=int(flops), bytes_accessed=int(nbytes), transcendentals=0)


SMEM = pl.BlockSpec(memory_space=pltpu.SMEM)
HBM = pl.BlockSpec(memory_space=pltpu.HBM)
INVMEM = pl.BlockSpec(memory_space=pltpu.VMEM)


def shape_of(shape, kind=F32):
    return jax.ShapeDtypeStruct(shape, kind)


def call(kernel, name, arrays, in_specs, outs, out_specs, flops, scratch=(), limit=58):
    moved = sum(x.nbytes for x in arrays) + sum(x.size * x.dtype.itemsize for x in outs)
    return pl.pallas_call(
        kernel,
        in_specs=in_specs,
        out_specs=out_specs,
        out_shape=outs,
        scratch_shapes=list(scratch),
        compiler_params=pltpu.CompilerParams(vmem_limit_bytes=limit * MIB),
        cost_estimate=cost(flops, moved),
        name=name,
    )(*arrays)


def chunk(src, dst, sems, i):
    at = pl.ds(i * CHUNK, CHUNK)
    return pltpu.make_async_copy(src.at[at], dst.at[at], sems.at[i])


def loop(count, body):
    def one(i, _):
        body(i)
        return 0

    lax.fori_loop(0, count, one, 0)


def stacked(c):
    h = c.astype(BF16).astype(F32)
    pad = jnp.zeros((-3 * c.shape[0] % 16, c.shape[1]), F32)
    return jnp.concatenate([h, c - h, h, pad], axis=0).astype(BF16)


def correction(ret, width, t):
    at = lax.div(t, TILES) * width + lax.rem(t, TILES)
    return jnp.concatenate([ret[at], ret[at + 1]], axis=1)


def gathered(find, cpos, nbr, n):
    tiles = []
    for k in range(5):
        tiles.append(find(cpos[n] if k == 0 else cpos[nbr[n * 4 + k - 1]]))
    return stacked(jnp.concatenate(tiles, axis=0))


def alpha_of(ret):
    width = TILES + 1
    total = ret[TILES]
    for q in range(1, ret.shape[0] // width):
        total = total + ret[q * width + TILES]
    return total[0:1, 0:1] / total[1:2, 0:1]


def invert(pick, inv):
    def put(q, _):
        inv[pick[q]] = q
        return 0

    lax.fori_loop(0, pick.shape[0], put, 0)


def first_kernel(pick, r_ref, p_ref, send_ref, inv_ref, r, slots, sems, out_sems):
    nb = r.shape[0]
    for i in range(nb // CHUNK):
        chunk(r_ref, r, sems, i).start()
    invert(pick, inv_ref)

    def some(i):
        chunk(r_ref, r, sems, i).wait()
        for j in range(CHUNK):
            n = i * CHUNK + j
            slots[inv_ref[n]] = fold_rows(nt(rows_by(p_ref[n]), wide(r[n])))

    loop(nb // CHUNK, some)
    copies = [
        pltpu.make_async_copy(slots, send_ref.at[g], out_sems.at[g])
        for g in range(send_ref.shape[0])
    ]
    for c in copies:
        c.start()
    for c in copies:
        c.wait()


def first_rhs(pick, r, p, groups):
    nb, nr, b = r.shape
    nc = p.shape[1]
    return call(
        first_kernel,
        "first_rhs",
        [pick, r, p],
        [SMEM, HBM, INVMEM],
        [shape_of((groups, nb, nc, nr)), shape_of((nb,), jnp.int32)],
        [HBM, SMEM],
        2 * 16 * 256 * 256 * nb,
        [
            pltpu.VMEM(r.shape, F32),
            pltpu.VMEM((nb, nc, nr), F32),
            pltpu.SemaphoreType.DMA((nb // CHUNK,)),
            pltpu.SemaphoreType.DMA((groups,)),
        ],
    )


def fine_block(v, f):
    inner = fold(nn(wide(v), weights_nn(f)))
    return fold(nt(wide(inner), weights_nt(f)))


def fine_first_kernel(send, inv, v_hbm, fac_hbm, p_ref, f_hbm, out_ref, v, fac, ext, v_sem, fac_sem, f_sem):
    steps = v.shape[0] // CHUNK
    nr = v.shape[1]
    nc = p_ref.shape[1]
    for i in range(steps):
        chunk(v_hbm, v, v_sem, i).start()
        chunk(fac_hbm, fac, fac_sem, i).start()

    def some(i):
        chunk(v_hbm, v, v_sem, i).wait()
        chunk(fac_hbm, fac, fac_sem, i).wait()
        for j in range(CHUNK):
            n = i * CHUNK + j
            ext[n] = wide(fine_block(v[n], fac[n]))
        chunk(ext, f_hbm, f_sem, i).start()

    loop(steps, some)
    for j in range(send.shape[0]):
        n = send[j]
        out_ref[j, :nr] = fold(ext[n].astype(F32))
        out_ref[j, nr : nr + nc] = p_ref[n]
        out_ref[j, nr + nc :] = jnp.full((8, p_ref.shape[2]), inv[n].astype(F32))
    for i in range(steps):
        chunk(ext, f_hbm, f_sem, i).wait()


def fine_first(send, inv, v, fac, p):
    nb, nr, b = v.shape
    nc = p.shape[1]
    return call(
        fine_first_kernel,
        "fine_first",
        [send, inv, v, fac, p],
        [SMEM, SMEM, HBM, HBM, INVMEM],
        [shape_of((nb, nr, 2 * b), BF16), shape_of((send.shape[0], nr + nc + 8, b))],
        [HBM, INVMEM],
        4 * 256**3 * nb,
        [
            pltpu.VMEM(v.shape, F32),
            pltpu.VMEM(fac.shape, F32),
            pltpu.VMEM((nb, nr, 2 * b), BF16),
        ]
        + [pltpu.SemaphoreType.DMA((nb // CHUNK,))] * 3,
    )


def operator_kernel(nbr, f_hbm, lo_ref, up_ref, d_hbm, w_hbm, p_ref, *refs, setup, paf):
    refs = list(refs)
    af_hbm = refs.pop(0)
    paf_ref = refs.pop(0) if paf else None
    if setup:
        g_ref, h_ref, pext, grows = refs[:2] + refs[-2:]
        refs = refs[2:-2]
    d, w, ext, kept, d_sem, w_sem, f_sem, af_sem = refs
    nb, nr, b = kept.shape
    nc = p_ref.shape[1]
    halo = lo_ref.shape[0]
    steps = nb // CHUNK

    for i in range(steps):
        chunk(f_hbm, ext, f_sem, i).start()
    for i in range(steps):
        chunk(d_hbm, d, d_sem, i).start()
        chunk(w_hbm, w, w_sem, i).start()
    for j in range(halo):
        ext[nb + j] = wide(lo_ref[j, :nr])
        ext[nb + halo + j] = wide(up_ref[j, :nr])
    if setup:
        pext[pl.ds(0, nb)] = p_ref[...]
        pext[pl.ds(nb, halo)] = lo_ref[:, nr : nr + nc]
        pext[pl.ds(nb + halo, halo)] = up_ref[:, nr : nr + nc]
    for i in range(steps):
        chunk(f_hbm, ext, f_sem, i).wait()

    def products(i):
        for j in range(CHUNK):
            n = i * CHUNK + j
            p = p_ref[n]
            paf_ref[n] = fold_rows(nt(wide(kept[n]), rows_by(p)).T)
            if setup:
                g = grows[n]
                gh = g.astype(BF16).astype(F32)
                pad = jnp.zeros((8, g.shape[1]), F32)
                g_ref[n] = jnp.concatenate([gh, gh, g - gh, pad], axis=0).astype(BF16)
                thrice = jnp.concatenate([g, g, g, pad], axis=0)
                h = fold_rows(nt(rows_by(p), wide(thrice)))
                hh = h.astype(BF16).astype(F32)
                lane = lax.broadcasted_iota(jnp.int32, h.shape, 1)
                h_ref[n] = jnp.where(lane < 80, hh, h - hh)

    def image(i):
        chunk(d_hbm, d, d_sem, i).wait()
        chunk(w_hbm, w, w_sem, i).wait()
        if paf and i:
            products(i - 1)
        for j in range(CHUNK):
            n = i * CHUNK + j
            fields = []
            weights = []
            rows = []
            for k in range(5):
                e = n if k == 0 else nbr[n * 4 + k - 1]
                weights.append(weights_nt(d[n] if k == 0 else w[n, k - 1]))
                fields.append(ext[e])
                if setup:
                    p = pext[e]
                    ph = p.astype(BF16).astype(F32)
                    row = [jnp.zeros((nc, 2 * b), F32)] * 5
                    row[k] = jnp.concatenate([ph, p - ph], axis=1)
                    rows.append(jnp.concatenate(row, axis=1))
            lhs = jnp.concatenate(fields, axis=1)
            if setup:
                rows = jnp.concatenate(rows + [jnp.zeros_like(rows[0])], axis=0).astype(BF16)
                lhs = jnp.concatenate([lhs, rows], axis=0)
            got = fold(nt(lhs, jnp.concatenate(weights, axis=1)))
            if setup:
                grows[n] = got[nr : nr + 5 * nc]
                got = got[:nr]
            kept[n] = got
        chunk(kept, af_hbm, af_sem, i).start()

    for i in range(steps):
        image(i)
    if paf:
        products(steps - 1)
    for i in range(steps):
        chunk(kept, af_hbm, af_sem, i).wait()


def operator(nbr, f, lo, up, d, w, p, setup=False, paf=True):
    nb, nc, b = p.shape
    nr = f.shape[1]
    places = nb + 2 * lo.shape[0]
    outs = [shape_of((nb, nr, b))]
    scratch = [pltpu.VMEM(d.shape, F32), pltpu.VMEM(w.shape, F32)]
    scratch += [pltpu.VMEM((places, nr, 2 * b), BF16), pltpu.VMEM((nb, nr, b), F32)]
    scratch += [pltpu.SemaphoreType.DMA((nb // CHUNK,))] * 4
    if paf:
        outs.append(shape_of((nb, nc, nr)))
    if setup:
        outs += [shape_of((nb, b, b), BF16), shape_of((nb, nc, b))]
        scratch += [pltpu.VMEM((places, nc, b), F32), pltpu.VMEM((nb, 5 * nc, b), F32)]
    return call(
        functools.partial(operator_kernel, setup=setup, paf=paf),
        "operator",
        [nbr, f, lo, up, d, w, p],
        [SMEM, HBM, INVMEM, INVMEM, HBM, HBM, INVMEM],
        outs,
        [HBM] + [INVMEM] * (len(outs) - 1),
        10 * 256**3 * nb,
        scratch,
        53,
    )


def solve_kernel(v_ref, c_ref, *refs):
    *sums, out_ref, res, sem = refs
    vh, vl = parts(v_ref[...])
    ch, cl = parts(c_ref[0])
    sol = nn(ch, vh) + nn(ch, vl) + nn(cl, vh)
    ns = res.shape[0]
    half = sol.shape[1] // 2
    if sums:
        total = sums[0][...] + sums[1][...] + sums[2][...] + sums[3][...]
    for s in range(ns):
        rows = sol[8 * s : 8 * s + 8]
        for place, to in ((0, s), (1, (s + 1) % ns), (2, (s - 1) % ns)):
            res[to, 2 * place] = rows[:, :half]
            res[to, 2 * place + 1] = rows[:, half:]
        if sums:
            res[s, TILES] = total
    out = pltpu.make_async_copy(res, out_ref, sem)
    out.start()
    out.wait()


def solve(vec, inverse, ns, sums):
    k, nr = vec.shape
    shape = (ns, TILES + (1 if sums else 0), 8, nr // 2)
    return call(
        solve_kernel,
        "coarse_solve",
        [vec, inverse, *sums],
        [INVMEM, INVMEM] + [INVMEM] * len(sums),
        [shape_of(shape)],
        [HBM],
        2 * 3 * 256 * k * nr,
        [pltpu.VMEM(shape, F32), pltpu.SemaphoreType.DMA],
        24,
    )[0]


def next_kernel(pick, cpos, nbr, ret_ref, paf_ref, h_ref, *refs, width):
    nb = paf_ref.shape[0]
    send_ref, slots, sems = refs
    groups = send_ref.shape[0]

    def out(i, g):
        at = pl.ds(i * CHUNK, CHUNK)
        return pltpu.make_async_copy(slots.at[at], send_ref.at[g, at], sems.at[g, i])

    def some(i):
        for j in range(CHUNK):
            q = i * CHUNK + j
            n = pick[q]
            c = gathered(lambda t: correction(ret_ref, width, t), cpos, nbr, n)
            slots[q] = paf_ref[n] + nn(h_ref[n].astype(BF16), c)
        for g in range(groups):
            out(i, g).start()

    loop(nb // CHUNK, some)
    for i in range(nb // CHUNK):
        for g in range(groups):
            out(i, g).wait()


def next_rhs(pick, cpos, nbr, ret, width, paf, h, groups):
    nb, nc, nr = paf.shape
    return call(
        functools.partial(next_kernel, width=width),
        "next_rhs",
        [pick, cpos, nbr, ret, paf, h],
        [SMEM] * 3 + [INVMEM] * 3,
        [shape_of((groups, nb, nc, nr))],
        [HBM],
        2 * 16 * 256 * 128 * nb,
        [pltpu.VMEM((nb, nc, nr), F32), pltpu.SemaphoreType.DMA((groups, nb // CHUNK))],
        24,
    )


def image_kernel(cpos, nbr, *refs, stage, widths):
    refs = list(refs)

    def take(count):
        found = refs[:count]
        del refs[:count]
        return found

    send = None if stage == 2 else refs.pop(0)
    rets = take(2 if stage == 2 else 1)
    g_hbm, af_hbm, r_hbm = take(3)
    old_hbm = refs.pop(0) if stage else None
    fac_hbm = None if stage == 2 else refs.pop(0)
    before_ref = refs.pop(0) if stage == 2 else None
    w_out = refs.pop(0)
    r_out = refs.pop(0) if stage == 1 else None
    if stage == 2:
        kept_r = refs.pop(0)
    f_out = None if stage == 2 else refs.pop(0)
    sum_ref = refs.pop(0)
    sent_ref = None if stage == 2 else refs.pop(0)
    if stage == 2:
        af, r = w_out, kept_r
        g, old, af_sem, r_sem, g_sem, old_sem = take(6)
    else:
        af, r, g, af_sem, r_sem, g_sem, w_sem = take(7)
        if stage:
            old, old_sem = take(2)
    if stage < 2:
        fac, ext, fac_sem, r_out_sem, f_sem = take(5)
    nb = af.shape[0]
    steps = nb // CHUNK

    def ins(i):
        found = [chunk(af_hbm, af, af_sem, i), chunk(r_hbm, r, r_sem, i), chunk(g_hbm, g, g_sem, i)]
        if stage:
            found.append(chunk(old_hbm, old, old_sem, i))
        if stage < 2:
            found.append(chunk(fac_hbm, fac, fac_sem, i))
        return found

    def outs(i):
        if stage == 2:
            return []
        found = [chunk(af, w_out, w_sem, i)]
        if stage == 1:
            found.append(chunk(r, r_out, r_out_sem, i))
        return found

    for i in range(steps):
        for c in ins(i):
            c.start()
    alpha = alpha_of(rets[0]) if stage else None

    def find(t):
        c = correction(rets[0], widths[0], t)
        if stage == 2:
            c = c - alpha * correction(rets[1], widths[1], t)
        return c

    def fine(i):
        for j in range(CHUNK):
            n = i * CHUNK + j
            ext[n] = wide(fine_block(af[n], fac[n]))
        chunk(ext, f_out, f_sem, i).start()

    def some(i, acc):
        acc = list(acc)
        for c in ins(i):
            c.wait()
        for j in range(CHUNK):
            n = i * CHUNK + j
            w = af[n] + tn(gathered(find, cpos, nbr, n), g[n])
            res = r[n]
            if stage == 0:
                pairs = ((w, res), (w, w))
            elif stage == 1:
                before = old[n]
                w = before - alpha * w
                res = res - alpha * before
                r[n] = res
                pairs = ((w, res), (w, w))
            else:
                pairs = ((w, res), (w, w), (w, old[n]))
            af[n] = w
            for k, (x, y) in enumerate(pairs):
                acc[k] += jnp.sum((x * y).reshape(-1, 8, w.shape[1]), axis=0)
        if stage < 2 and i:
            fine(i - 1)
        for c in outs(i):
            c.start()
        return acc

    zero = jnp.zeros((8, af.shape[2]), F32)
    acc = [zero] * (3 if stage == 2 else 2)
    for i in range(steps):
        acc = some(i, acc)
    acc = [jnp.sum(x, keepdims=True) for x in acc]
    shape = (2, af.shape[2]) if stage == 2 else sum_ref.shape
    row = lax.broadcasted_iota(jnp.int32, shape, 1 if stage == 2 else 0)
    if stage == 2:
        acc += [before_ref[0:1, 0:1], before_ref[1:2, 0:1]]
    total = jnp.zeros(shape, F32)
    for k, x in enumerate(acc):
        total = jnp.where(row == k, x, total)
    if stage == 2:
        for k in range(sum_ref.shape[0]):
            sum_ref[k] = total
    else:
        sum_ref[...] = total
        fine(steps - 1)
        for j in range(send.shape[0]):
            sent_ref[j] = fold(ext[send[j]].astype(F32))
        for i in range(steps):
            chunk(ext, f_out, f_sem, i).wait()
    for i in range(steps):
        for c in outs(i):
            c.wait()


def image_of(stage, cpos, nbr, rets, widths, g, af, r, old=None, send=None, fac=None, before=None, everyone=0):
    nb, nr, b = af.shape
    steps = nb // CHUNK
    dma = pltpu.SemaphoreType.DMA
    ins = [cpos, nbr] + ([] if send is None else [send])
    specs = [SMEM] * len(ins)
    ins += [*rets, g, af, r]
    specs += [INVMEM] * len(rets) + [HBM] * 3
    scratch = [pltpu.VMEM(g.shape, BF16)]
    if stage < 2:
        scratch = [pltpu.VMEM(af.shape, F32)] * 2 + scratch
    else:
        scratch.append(pltpu.VMEM(af.shape, F32))
    scratch += [dma((steps,))] * 4
    if stage:
        ins.append(old)
        specs.append(HBM)
    if stage == 1:
        scratch += [pltpu.VMEM(af.shape, F32), dma((steps,))]
    outs = [shape_of(af.shape)] * (2 if stage else 1)
    if stage < 2:
        outs.append(shape_of((nb, nr, 2 * b), BF16))
    out_specs = [HBM if stage < 2 else INVMEM] * len(outs)
    if stage < 2:
        count = send.shape[0]
        ins.append(fac)
        specs.append(HBM)
        outs += [shape_of((8, b)), shape_of((count, nr, b))]
        scratch += [pltpu.VMEM(fac.shape, F32), pltpu.VMEM((nb, nr, 2 * b), BF16)]
        scratch += [dma((steps,))] * 3
    else:
        ins.append(before)
        specs.append(INVMEM)
        outs.append(shape_of((everyone, 2, b)))
    out_specs += [INVMEM] * (len(outs) - len(out_specs))
    return call(
        functools.partial(image_kernel, stage=stage, widths=widths),
        "image",
        ins,
        specs,
        outs,
        out_specs,
        2 * 256 * 128 * 128 * nb,
        scratch,
        58 if stage < 2 else 50,
    )


def final_kernel(cpos, *refs, widths):
    sum_ref, rets, p_ref = refs[0], refs[1:4], refs[4]
    hbms, (r, y), (s_hbm, r_hbm) = refs[5:9], refs[9:11], refs[11:13]
    s, res, *refs = refs[13:]
    bufs, (s_sem, r_sem), sems = refs[:4], refs[4:6], refs[6:]
    fs, w = bufs[:3], bufs[3]
    nb = p_ref.shape[0]
    for i in range(nb // CHUNK):
        for k in range(4):
            chunk(hbms[k], bufs[k], sems[k], i).start()
    total = jnp.sum(sum_ref[...], axis=0)
    yr, yy, yw, wr, ww = (total[0:1, k : k + 1] for k in range(5))
    a0 = alpha_of(rets[1])
    a1 = wr / ww
    a2 = (wr - a1 * ww - a1 * yr + a1 * a1 * yw) / (ww - 2.0 * a1 * yw + a1 * a1 * yy)
    b0 = a0 + a1 + a2
    b1 = -a0 * (a1 + a2)
    b2 = -a1 * a2

    def some(i):
        for k in range(4):
            chunk(hbms[k], bufs[k], sems[k], i).wait()
        for j in range(CHUNK):
            n = i * CHUNK + j
            p = p_ref[n]
            ph = p.astype(BF16).astype(F32)
            p3 = jnp.concatenate([ph, ph, p - ph, jnp.zeros_like(p)], axis=0).astype(BF16)
            c0, c1, cy = (correction(x, k, cpos[n]) for x, k in zip(rets, widths))
            c = b0 * c0 + (b1 + b2) * c1 - b2 * a0 * cy
            f0, f1, f2 = (fold(x[n].astype(F32)) for x in fs)
            s[n] = b0 * f0 + b1 * f1 + b2 * f2 + tn(stacked(c), p3)
            res[n] = r[n] - (a1 + a2) * w[n] + a1 * a2 * y[n]
        chunk(s, s_hbm, s_sem, i).start()
        chunk(res, r_hbm, r_sem, i).start()

    loop(nb // CHUNK, some)
    for i in range(nb // CHUNK):
        chunk(s, s_hbm, s_sem, i).wait()
        chunk(res, r_hbm, r_sem, i).wait()


def final(cpos, sums, rets, widths, p, fs, w, r, y):
    nb = p.shape[0]
    return call(
        functools.partial(final_kernel, widths=widths),
        "final",
        [cpos, sums, *rets, p, *fs, w, r, y],
        [SMEM] + [INVMEM] * 5 + [HBM] * 4 + [INVMEM] * 2,
        [shape_of(w.shape)] * 2,
        [HBM, HBM],
        2 * 256 * 128 * 128 * nb,
        [pltpu.VMEM(w.shape, F32)] * 2
        + [pltpu.VMEM(x.shape, x.dtype) for x in (*fs, w)]
        + [pltpu.SemaphoreType.DMA((nb // CHUNK,))] * 6,
        48,
    )


def shifted(x, axis, by):
    count = lax.axis_size(axis)
    return lax.ppermute(x, axis, [(i, (i + by) % count) for i in range(count)])


def both_ways(x):
    return shifted(x, "sub", 1), shifted(x, "sub", -1)


def local(
    right_side,
    diag_blocks,
    couplings,
    factors,
    prolong,
    coarse_inverse,
    intersection_send,
    neighbours,
    coarse_pick,
):
    nb, nr, b = right_side.shape
    nc = prolong.shape[1]
    ns = lax.axis_size("sub")
    ng = lax.axis_size("grp")
    nbr = neighbours.reshape(-1)

    def exchange(send):
        flat = send.reshape(ng * nb, nc, nr)
        got = lax.all_to_all(flat, ("grp", "sub"), split_axis=0, concat_axis=0, tiled=True)
        return got.reshape(ng * nb * nc, nr)

    def coarse(vec, *sums):
        out = solve(vec, coarse_inverse, ns, sums)
        back = lax.all_to_all(out, "sub", split_axis=0, concat_axis=0, tiled=True)
        return back.reshape(-1, 8, nr // 2)

    def places(x):
        return x[:, nr + nc, 0].astype(jnp.int32) * TILES

    weights = (diag_blocks, couplings, prolong)
    widths = (TILES, TILES + 1, TILES)
    send, inv = first_rhs(coarse_pick, right_side, prolong, ng)
    vec0 = exchange(send)
    f0, sent = fine_first(intersection_send, inv, right_side, factors, prolong)
    lo, up = both_ways(sent)
    cpos = jnp.concatenate([inv * TILES, places(lo) + 2, places(up) + 4])
    af0, paf0, g, h = operator(nbr, f0, lo, up, *weights, setup=True)
    ret0 = coarse(vec0)

    (send,) = next_rhs(coarse_pick, cpos, nbr, ret0, widths[0], paf0, h, ng)
    vec1 = exchange(send)
    w0, f1, sums0, sent = image_of(
        0, cpos, nbr, [ret0], widths[:1], g, af0, right_side, send=intersection_send, fac=factors
    )
    lo, up = both_ways(sent)
    af1, paf1 = operator(nbr, f1, lo, up, *weights)
    ret1 = coarse(vec1, sums0, *(shifted(sums0, "grp", k) for k in range(1, ng)))

    (send,) = next_rhs(coarse_pick, cpos, nbr, ret1, widths[1], paf1, h, ng)
    vec2 = exchange(send)
    w1, r1, f2, sums1, sent = image_of(
        1, cpos, nbr, [ret1], widths[1:2], g, af1, right_side, w0, intersection_send, factors
    )
    lo, up = both_ways(sent)
    (af2,) = operator(nbr, f2, lo, up, *weights, paf=False)
    ret2 = coarse(vec2)

    y1, r1, sums = image_of(
        2, cpos, nbr, [ret1, ret2], widths[1:], g, af2, r1, w1, before=sums1, everyone=ns * ng
    )
    sums = lax.all_to_all(sums, ("grp", "sub"), split_axis=0, concat_axis=0, tiled=True)
    return final(cpos, sums, (ret0, ret1, ret2), widths, prolong, (f0, f1, f2), w1, r1, y1)


def solution(mesh):
    return jax.shard_map(
        local,
        mesh=mesh,
        in_specs=(
            P(("sub", "grp"), None, None),
            P(("sub", "grp"), None, None),
            P(("sub", "grp"), None, None, None),
            P(("sub", "grp"), None, None),
            P(("sub", "grp"), None, None),
            P("sub", "grp", None),
            P(("sub", "grp")),
            P(("sub", "grp"), None),
            P(("sub", "grp")),
        ),
        out_specs=(P(("sub", "grp"), None, None), P(("sub", "grp"), None, None)),
        check_vma=False,
    )
```

```python
import functools

import jax
import jax.numpy as jnp
from jax import lax
from jax.experimental import pallas as pl
from jax.experimental.pallas import tpu as pltpu
from jax.sharding import PartitionSpec as P

F32 = jnp.float32
BF16 = jnp.bfloat16
TILES = 6
MIB = 1024 * 1024
CHUNK = 8
AHEAD = 2


def nn(a, b):
    return lax.dot_general(a, b, (((1,), (0,)), ((), ())), preferred_element_type=F32)


def nt(a, b):
    return lax.dot_general(a, b, (((1,), (1,)), ((), ())), preferred_element_type=F32)


def tn(a, b):
    return lax.dot_general(a, b, (((0,), (0,)), ((), ())), preferred_element_type=F32)


def parts(x):
    head = x.astype(BF16)
    return head, (x - head.astype(F32)).astype(BF16)


def wide(x):
    return jnp.concatenate(parts(x), axis=1)


def fold(x):
    half = x.shape[1] // 2
    return x[:, :half] + x[:, half:]


def weights_nt(w):
    h, l = parts(w)
    return jnp.concatenate([jnp.concatenate([h, h], 1), jnp.concatenate([l, l], 1)], 0)


def weights_nn(w):
    h, l = parts(w)
    row = jnp.concatenate([h, l], 1)
    return jnp.concatenate([row, row], 0)


def rows_by(p):
    return weights_nt(p)


def fold_rows(x):
    half = x.shape[0] // 2
    return x[:half] + x[half:]


def cost(flops, nbytes):
    return pl.CostEstimate(flops=int(flops), bytes_accessed=int(nbytes), transcendentals=0)


SMEM = pl.BlockSpec(memory_space=pltpu.SMEM)
HBM = pl.BlockSpec(memory_space=pltpu.HBM)
INVMEM = pl.BlockSpec(memory_space=pltpu.VMEM)


def shape_of(shape, kind=F32):
    return jax.ShapeDtypeStruct(shape, kind)


def call(kernel, name, arrays, in_specs, outs, out_specs, flops, scratch=(), limit=58):
    moved = sum(x.nbytes for x in arrays) + sum(x.size * x.dtype.itemsize for x in outs)
    return pl.pallas_call(
        kernel,
        in_specs=in_specs,
        out_specs=out_specs,
        out_shape=outs,
        scratch_shapes=list(scratch),
        compiler_params=pltpu.CompilerParams(vmem_limit_bytes=limit * MIB),
        cost_estimate=cost(flops, moved),
        name=name,
    )(*arrays)


def chunk(src, dst, sems, i):
    at = pl.ds(i * CHUNK, CHUNK)
    return pltpu.make_async_copy(src.at[at], dst.at[at], sems.at[i])


def loop(count, body):
    def one(i, _):
        body(i)
        return 0

    lax.fori_loop(0, count, one, 0)


def stacked(c):
    h = c.astype(BF16).astype(F32)
    pad = jnp.zeros((-3 * c.shape[0] % 16, c.shape[1]), F32)
    return jnp.concatenate([h, c - h, h, pad], axis=0).astype(BF16)


def correction(ret, width, t):
    at = lax.div(t, TILES) * width + lax.rem(t, TILES)
    return jnp.concatenate([ret[at], ret[at + 1]], axis=1)


def gathered(find, cpos, nbr, n):
    tiles = []
    for k in range(5):
        tiles.append(find(cpos[n] if k == 0 else cpos[nbr[n * 4 + k - 1]]))
    return stacked(jnp.concatenate(tiles, axis=0))


def alpha_of(ret):
    width = TILES + 1
    total = ret[TILES]
    for q in range(1, ret.shape[0] // width):
        total = total + ret[q * width + TILES]
    return total[0:1, 0:1] / total[1:2, 0:1]


def invert(pick, inv):
    def put(q, _):
        inv[pick[q]] = q
        return 0

    lax.fori_loop(0, pick.shape[0], put, 0)


def first_kernel(pick, r_ref, p_ref, send_ref, inv_ref, r, slots, sems, out_sems):
    nb = r.shape[0]
    for i in range(nb // CHUNK):
        chunk(r_ref, r, sems, i).start()
    invert(pick, inv_ref)

    def some(i):
        chunk(r_ref, r, sems, i).wait()
        for j in range(CHUNK):
            n = i * CHUNK + j
            slots[inv_ref[n]] = fold_rows(nt(rows_by(p_ref[n]), wide(r[n])))

    loop(nb // CHUNK, some)
    copies = [
        pltpu.make_async_copy(slots, send_ref.at[g], out_sems.at[g])
        for g in range(send_ref.shape[0])
    ]
    for c in copies:
        c.start()
    for c in copies:
        c.wait()


def first_rhs(pick, r, p, groups):
    nb, nr, b = r.shape
    nc = p.shape[1]
    return call(
        first_kernel,
        "first_rhs",
        [pick, r, p],
        [SMEM, HBM, INVMEM],
        [shape_of((groups, nb, nc, nr)), shape_of((nb,), jnp.int32)],
        [HBM, SMEM],
        2 * 16 * 256 * 256 * nb,
        [
            pltpu.VMEM(r.shape, F32),
            pltpu.VMEM((nb, nc, nr), F32),
            pltpu.SemaphoreType.DMA((nb // CHUNK,)),
            pltpu.SemaphoreType.DMA((groups,)),
        ],
    )


def fine_block(v, f):
    inner = fold(nn(wide(v), weights_nn(f)))
    return fold(nt(wide(inner), weights_nt(f)))


def fine_first_kernel(send, inv, v_hbm, fac_hbm, p_ref, f_hbm, out_ref, v, fac, ext, v_sem, fac_sem, f_sem):
    steps = v.shape[0] // CHUNK
    nr = v.shape[1]
    nc = p_ref.shape[1]
    for i in range(steps):
        chunk(v_hbm, v, v_sem, i).start()
        chunk(fac_hbm, fac, fac_sem, i).start()

    def some(i):
        chunk(v_hbm, v, v_sem, i).wait()
        chunk(fac_hbm, fac, fac_sem, i).wait()
        for j in range(CHUNK):
            n = i * CHUNK + j
            ext[n] = wide(fine_block(v[n], fac[n]))
        chunk(ext, f_hbm, f_sem, i).start()

    loop(steps, some)
    for j in range(send.shape[0]):
        n = send[j]
        out_ref[j, :nr] = fold(ext[n].astype(F32))
        out_ref[j, nr : nr + nc] = p_ref[n]
        out_ref[j, nr + nc :] = jnp.full((8, p_ref.shape[2]), inv[n].astype(F32))
    for i in range(steps):
        chunk(ext, f_hbm, f_sem, i).wait()


def fine_first(send, inv, v, fac, p):
    nb, nr, b = v.shape
    nc = p.shape[1]
    return call(
        fine_first_kernel,
        "fine_first",
        [send, inv, v, fac, p],
        [SMEM, SMEM, HBM, HBM, INVMEM],
        [shape_of((nb, nr, 2 * b), BF16), shape_of((send.shape[0], nr + nc + 8, b))],
        [HBM, INVMEM],
        4 * 256**3 * nb,
        [
            pltpu.VMEM(v.shape, F32),
            pltpu.VMEM(fac.shape, F32),
            pltpu.VMEM((nb, nr, 2 * b), BF16),
        ]
        + [pltpu.SemaphoreType.DMA((nb // CHUNK,))] * 3,
    )


def operator_kernel(nbr, f_hbm, lo_ref, up_ref, d_hbm, w_hbm, p_ref, *refs, setup, paf):
    refs = list(refs)
    af_hbm = refs.pop(0)
    paf_ref = refs.pop(0) if paf else None
    if setup:
        g_ref, h_ref, pext, grows = refs[:2] + refs[-2:]
        refs = refs[2:-2]
    d, w, ext, kept, d_sem, w_sem, f_sem, af_sem = refs
    nb, nr, b = kept.shape
    nc = p_ref.shape[1]
    halo = lo_ref.shape[0]
    steps = nb // CHUNK

    for i in range(steps):
        chunk(f_hbm, ext, f_sem, i).start()

    def fetch(i):
        chunk(d_hbm, d, d_sem, i).start()
        chunk(w_hbm, w, w_sem, i).start()

    for i in range(AHEAD):
        fetch(i)
    for j in range(halo):
        ext[nb + j] = wide(lo_ref[j, :nr])
        ext[nb + halo + j] = wide(up_ref[j, :nr])
    if setup:
        pext[pl.ds(0, nb)] = p_ref[...]
        pext[pl.ds(nb, halo)] = lo_ref[:, nr : nr + nc]
        pext[pl.ds(nb + halo, halo)] = up_ref[:, nr : nr + nc]
    for i in range(steps):
        chunk(f_hbm, ext, f_sem, i).wait()

    def products(i):
        for j in range(CHUNK):
            n = i * CHUNK + j
            p = p_ref[n]
            paf_ref[n] = fold_rows(nt(wide(kept[n]), rows_by(p)).T)
            if setup:
                g = grows[n]
                gh = g.astype(BF16).astype(F32)
                pad = jnp.zeros((8, g.shape[1]), F32)
                g_ref[n] = jnp.concatenate([gh, gh, g - gh, pad], axis=0).astype(BF16)
                thrice = jnp.concatenate([g, g, g, pad], axis=0)
                h = fold_rows(nt(rows_by(p), wide(thrice)))
                hh = h.astype(BF16).astype(F32)
                lane = lax.broadcasted_iota(jnp.int32, h.shape, 1)
                h_ref[n] = jnp.where(lane < 80, hh, h - hh)

    def image(i):
        chunk(d_hbm, d, d_sem, i).wait()
        chunk(w_hbm, w, w_sem, i).wait()
        if i + AHEAD < steps:
            fetch(i + AHEAD)
        if paf and i:
            products(i - 1)
        for j in range(CHUNK):
            n = i * CHUNK + j
            fields = []
            weights = []
            rows = []
            for k in range(5):
                e = n if k == 0 else nbr[n * 4 + k - 1]
                weights.append(weights_nt(d[n] if k == 0 else w[n, k - 1]))
                fields.append(ext[e])
                if setup:
                    p = pext[e]
                    ph = p.astype(BF16).astype(F32)
                    row = [jnp.zeros((nc, 2 * b), F32)] * 5
                    row[k] = jnp.concatenate([ph, p - ph], axis=1)
                    rows.append(jnp.concatenate(row, axis=1))
            lhs = jnp.concatenate(fields, axis=1)
            if setup:
                rows = jnp.concatenate(rows + [jnp.zeros_like(rows[0])], axis=0).astype(BF16)
                lhs = jnp.concatenate([lhs, rows], axis=0)
            got = fold(nt(lhs, jnp.concatenate(weights, axis=1)))
            if setup:
                grows[n] = got[nr : nr + 5 * nc]
                got = got[:nr]
            kept[n] = got
        chunk(kept, af_hbm, af_sem, i).start()

    for i in range(steps):
        image(i)
    if paf:
        products(steps - 1)
    for i in range(steps):
        chunk(kept, af_hbm, af_sem, i).wait()


def operator(nbr, f, lo, up, d, w, p, setup=False, paf=True):
    nb, nc, b = p.shape
    nr = f.shape[1]
    places = nb + 2 * lo.shape[0]
    outs = [shape_of((nb, nr, b))]
    scratch = [pltpu.VMEM(d.shape, F32), pltpu.VMEM(w.shape, F32)]
    scratch += [pltpu.VMEM((places, nr, 2 * b), BF16), pltpu.VMEM((nb, nr, b), F32)]
    scratch += [pltpu.SemaphoreType.DMA((nb // CHUNK,))] * 4
    if paf:
        outs.append(shape_of((nb, nc, nr)))
    if setup:
        outs += [shape_of((nb, b, b), BF16), shape_of((nb, nc, b))]
        scratch += [pltpu.VMEM((places, nc, b), F32), pltpu.VMEM((nb, 5 * nc, b), F32)]
    return call(
        functools.partial(operator_kernel, setup=setup, paf=paf),
        "operator",
        [nbr, f, lo, up, d, w, p],
        [SMEM, HBM, INVMEM, INVMEM, HBM, HBM, INVMEM],
        outs,
        [HBM] + [INVMEM] * (len(outs) - 1),
        10 * 256**3 * nb,
        scratch,
        53,
    )


def solve_kernel(v_ref, c_ref, *refs):
    *sums, out_ref, res, sem = refs
    vh, vl = parts(v_ref[...])
    ch, cl = parts(c_ref[0])
    sol = nn(ch, vh) + nn(ch, vl) + nn(cl, vh)
    ns = res.shape[0]
    half = sol.shape[1] // 2
    if sums:
        total = sums[0][...] + sums[1][...] + sums[2][...] + sums[3][...]
    for s in range(ns):
        rows = sol[8 * s : 8 * s + 8]
        for place, to in ((0, s), (1, (s + 1) % ns), (2, (s - 1) % ns)):
            res[to, 2 * place] = rows[:, :half]
            res[to, 2 * place + 1] = rows[:, half:]
        if sums:
            res[s, TILES] = total
    out = pltpu.make_async_copy(res, out_ref, sem)
    out.start()
    out.wait()


def solve(vec, inverse, ns, sums):
    k, nr = vec.shape
    shape = (ns, TILES + (1 if sums else 0), 8, nr // 2)
    return call(
        solve_kernel,
        "coarse_solve",
        [vec, inverse, *sums],
        [INVMEM, INVMEM] + [INVMEM] * len(sums),
        [shape_of(shape)],
        [HBM],
        2 * 3 * 256 * k * nr,
        [pltpu.VMEM(shape, F32), pltpu.SemaphoreType.DMA],
        24,
    )[0]


def next_kernel(pick, cpos, nbr, ret_ref, paf_ref, h_ref, *refs, width):
    nb = paf_ref.shape[0]
    send_ref, slots, sems = refs
    groups = send_ref.shape[0]

    def out(i, g):
        at = pl.ds(i * CHUNK, CHUNK)
        return pltpu.make_async_copy(slots.at[at], send_ref.at[g, at], sems.at[g, i])

    def some(i):
        for j in range(CHUNK):
            q = i * CHUNK + j
            n = pick[q]
            c = gathered(lambda t: correction(ret_ref, width, t), cpos, nbr, n)
            slots[q] = paf_ref[n] + nn(h_ref[n].astype(BF16), c)
        for g in range(groups):
            out(i, g).start()

    loop(nb // CHUNK, some)
    for i in range(nb // CHUNK):
        for g in range(groups):
            out(i, g).wait()


def next_rhs(pick, cpos, nbr, ret, width, paf, h, groups):
    nb, nc, nr = paf.shape
    return call(
        functools.partial(next_kernel, width=width),
        "next_rhs",
        [pick, cpos, nbr, ret, paf, h],
        [SMEM] * 3 + [INVMEM] * 3,
        [shape_of((groups, nb, nc, nr))],
        [HBM],
        2 * 16 * 256 * 128 * nb,
        [pltpu.VMEM((nb, nc, nr), F32), pltpu.SemaphoreType.DMA((groups, nb // CHUNK))],
        24,
    )


def image_kernel(cpos, nbr, *refs, stage, widths):
    refs = list(refs)

    def take(count):
        found = refs[:count]
        del refs[:count]
        return found

    send = None if stage == 2 else refs.pop(0)
    rets = take(2 if stage == 2 else 1)
    g_hbm, af_hbm, r_hbm = take(3)
    old_hbm = refs.pop(0) if stage else None
    fac_hbm = None if stage == 2 else refs.pop(0)
    before_ref = refs.pop(0) if stage == 2 else None
    w_out = refs.pop(0)
    r_out = refs.pop(0) if stage == 1 else None
    if stage == 2:
        kept_r = refs.pop(0)
    f_out = None if stage == 2 else refs.pop(0)
    sum_ref = refs.pop(0)
    sent_ref = None if stage == 2 else refs.pop(0)
    if stage == 2:
        af, r = w_out, kept_r
        g, old, af_sem, r_sem, g_sem, old_sem = take(6)
    else:
        af, r, g, af_sem, r_sem, g_sem, w_sem = take(7)
        if stage:
            old, old_sem = take(2)
    if stage < 2:
        fac, ext, fac_sem, r_out_sem, f_sem = take(5)
    nb = af.shape[0]
    steps = nb // CHUNK

    def ins(i):
        found = [chunk(af_hbm, af, af_sem, i), chunk(r_hbm, r, r_sem, i), chunk(g_hbm, g, g_sem, i)]
        if stage:
            found.append(chunk(old_hbm, old, old_sem, i))
        if stage < 2:
            found.append(chunk(fac_hbm, fac, fac_sem, i))
        return found

    def outs(i):
        if stage == 2:
            return []
        found = [chunk(af, w_out, w_sem, i)]
        if stage == 1:
            found.append(chunk(r, r_out, r_out_sem, i))
        return found

    for i in range(steps):
        for c in ins(i):
            c.start()
    alpha = alpha_of(rets[0]) if stage else None

    def find(t):
        c = correction(rets[0], widths[0], t)
        if stage == 2:
            c = c - alpha * correction(rets[1], widths[1], t)
        return c

    def fine(i):
        for j in range(CHUNK):
            n = i * CHUNK + j
            ext[n] = wide(fine_block(af[n], fac[n]))
        chunk(ext, f_out, f_sem, i).start()

    def some(i, acc):
        acc = list(acc)
        for c in ins(i):
            c.wait()
        for j in range(CHUNK):
            n = i * CHUNK + j
            w = af[n] + tn(gathered(find, cpos, nbr, n), g[n])
            res = r[n]
            if stage == 0:
                pairs = ((w, res), (w, w))
            elif stage == 1:
                before = old[n]
                w = before - alpha * w
                res = res - alpha * before
                r[n] = res
                pairs = ((w, res), (w, w))
            else:
                pairs = ((w, res), (w, w), (w, old[n]))
            af[n] = w
            for k, (x, y) in enumerate(pairs):
                acc[k] += jnp.sum((x * y).reshape(-1, 8, w.shape[1]), axis=0)
        if stage < 2 and i:
            fine(i - 1)
        for c in outs(i):
            c.start()
        return acc

    zero = jnp.zeros((8, af.shape[2]), F32)
    acc = [zero] * (3 if stage == 2 else 2)
    for i in range(steps):
        acc = some(i, acc)
    acc = [jnp.sum(x, keepdims=True) for x in acc]
    shape = (2, af.shape[2]) if stage == 2 else sum_ref.shape
    row = lax.broadcasted_iota(jnp.int32, shape, 1 if stage == 2 else 0)
    if stage == 2:
        acc += [before_ref[0:1, 0:1], before_ref[1:2, 0:1]]
    total = jnp.zeros(shape, F32)
    for k, x in enumerate(acc):
        total = jnp.where(row == k, x, total)
    if stage == 2:
        for k in range(sum_ref.shape[0]):
            sum_ref[k] = total
    else:
        sum_ref[...] = total
        fine(steps - 1)
        for j in range(send.shape[0]):
            sent_ref[j] = fold(ext[send[j]].astype(F32))
        for i in range(steps):
            chunk(ext, f_out, f_sem, i).wait()
    for i in range(steps):
        for c in outs(i):
            c.wait()


def image_of(stage, cpos, nbr, rets, widths, g, af, r, old=None, send=None, fac=None, before=None, everyone=0):
    nb, nr, b = af.shape
    steps = nb // CHUNK
    dma = pltpu.SemaphoreType.DMA
    ins = [cpos, nbr] + ([] if send is None else [send])
    specs = [SMEM] * len(ins)
    ins += [*rets, g, af, r]
    specs += [INVMEM] * len(rets) + [HBM] * 3
    scratch = [pltpu.VMEM(g.shape, BF16)]
    if stage < 2:
        scratch = [pltpu.VMEM(af.shape, F32)] * 2 + scratch
    else:
        scratch.append(pltpu.VMEM(af.shape, F32))
    scratch += [dma((steps,))] * 4
    if stage:
        ins.append(old)
        specs.append(HBM)
    if stage == 1:
        scratch += [pltpu.VMEM(af.shape, F32), dma((steps,))]
    outs = [shape_of(af.shape)] * (2 if stage else 1)
    if stage < 2:
        outs.append(shape_of((nb, nr, 2 * b), BF16))
    out_specs = [HBM if stage < 2 else INVMEM] * len(outs)
    if stage < 2:
        count = send.shape[0]
        ins.append(fac)
        specs.append(HBM)
        outs += [shape_of((8, b)), shape_of((count, nr, b))]
        scratch += [pltpu.VMEM(fac.shape, F32), pltpu.VMEM((nb, nr, 2 * b), BF16)]
        scratch += [dma((steps,))] * 3
    else:
        ins.append(before)
        specs.append(INVMEM)
        outs.append(shape_of((everyone, 2, b)))
    out_specs += [INVMEM] * (len(outs) - len(out_specs))
    return call(
        functools.partial(image_kernel, stage=stage, widths=widths),
        "image",
        ins,
        specs,
        outs,
        out_specs,
        2 * 256 * 128 * 128 * nb,
        scratch,
        58 if stage < 2 else 50,
    )


def final_kernel(cpos, *refs, widths):
    sum_ref, rets, p_ref = refs[0], refs[1:4], refs[4]
    hbms, (r, y), (s_hbm, r_hbm) = refs[5:9], refs[9:11], refs[11:13]
    s, res, *refs = refs[13:]
    bufs, (s_sem, r_sem), sems = refs[:4], refs[4:6], refs[6:]
    fs, w = bufs[:3], bufs[3]
    nb = p_ref.shape[0]
    for i in range(nb // CHUNK):
        for k in range(4):
            chunk(hbms[k], bufs[k], sems[k], i).start()
    total = jnp.sum(sum_ref[...], axis=0)
    yr, yy, yw, wr, ww = (total[0:1, k : k + 1] for k in range(5))
    a0 = alpha_of(rets[1])
    a1 = wr / ww
    a2 = (wr - a1 * ww - a1 * yr + a1 * a1 * yw) / (ww - 2.0 * a1 * yw + a1 * a1 * yy)
    b0 = a0 + a1 + a2
    b1 = -a0 * (a1 + a2)
    b2 = -a1 * a2

    def some(i):
        for k in range(4):
            chunk(hbms[k], bufs[k], sems[k], i).wait()
        for j in range(CHUNK):
            n = i * CHUNK + j
            p = p_ref[n]
            ph = p.astype(BF16).astype(F32)
            p3 = jnp.concatenate([ph, ph, p - ph, jnp.zeros_like(p)], axis=0).astype(BF16)
            c0, c1, cy = (correction(x, k, cpos[n]) for x, k in zip(rets, widths))
            c = b0 * c0 + (b1 + b2) * c1 - b2 * a0 * cy
            f0, f1, f2 = (fold(x[n].astype(F32)) for x in fs)
            s[n] = b0 * f0 + b1 * f1 + b2 * f2 + tn(stacked(c), p3)
            res[n] = r[n] - (a1 + a2) * w[n] + a1 * a2 * y[n]
        chunk(s, s_hbm, s_sem, i).start()
        chunk(res, r_hbm, r_sem, i).start()

    loop(nb // CHUNK, some)
    for i in range(nb // CHUNK):
        chunk(s, s_hbm, s_sem, i).wait()
        chunk(res, r_hbm, r_sem, i).wait()


def final(cpos, sums, rets, widths, p, fs, w, r, y):
    nb = p.shape[0]
    return call(
        functools.partial(final_kernel, widths=widths),
        "final",
        [cpos, sums, *rets, p, *fs, w, r, y],
        [SMEM] + [INVMEM] * 5 + [HBM] * 4 + [INVMEM] * 2,
        [shape_of(w.shape)] * 2,
        [HBM, HBM],
        2 * 256 * 128 * 128 * nb,
        [pltpu.VMEM(w.shape, F32)] * 2
        + [pltpu.VMEM(x.shape, x.dtype) for x in (*fs, w)]
        + [pltpu.SemaphoreType.DMA((nb // CHUNK,))] * 6,
        48,
    )


def shifted(x, axis, by):
    count = lax.axis_size(axis)
    return lax.ppermute(x, axis, [(i, (i + by) % count) for i in range(count)])


def both_ways(x):
    return shifted(x, "sub", 1), shifted(x, "sub", -1)


def local(
    right_side,
    diag_blocks,
    couplings,
    factors,
    prolong,
    coarse_inverse,
    intersection_send,
    neighbours,
    coarse_pick,
):
    nb, nr, b = right_side.shape
    nc = prolong.shape[1]
    ns = lax.axis_size("sub")
    ng = lax.axis_size("grp")
    nbr = neighbours.reshape(-1)

    def exchange(send):
        flat = send.reshape(ng * nb, nc, nr)
        got = lax.all_to_all(flat, ("grp", "sub"), split_axis=0, concat_axis=0, tiled=True)
        return got.reshape(ng * nb * nc, nr)

    def coarse(vec, *sums):
        out = solve(vec, coarse_inverse, ns, sums)
        back = lax.all_to_all(out, "sub", split_axis=0, concat_axis=0, tiled=True)
        return back.reshape(-1, 8, nr // 2)

    def places(x):
        return x[:, nr + nc, 0].astype(jnp.int32) * TILES

    weights = (diag_blocks, couplings, prolong)
    widths = (TILES, TILES + 1, TILES)
    send, inv = first_rhs(coarse_pick, right_side, prolong, ng)
    vec0 = exchange(send)
    f0, sent = fine_first(intersection_send, inv, right_side, factors, prolong)
    lo, up = both_ways(sent)
    cpos = jnp.concatenate([inv * TILES, places(lo) + 2, places(up) + 4])
    af0, paf0, g, h = operator(nbr, f0, lo, up, *weights, setup=True)
    ret0 = coarse(vec0)

    (send,) = next_rhs(coarse_pick, cpos, nbr, ret0, widths[0], paf0, h, ng)
    vec1 = exchange(send)
    w0, f1, sums0, sent = image_of(
        0, cpos, nbr, [ret0], widths[:1], g, af0, right_side, send=intersection_send, fac=factors
    )
    lo, up = both_ways(sent)
    af1, paf1 = operator(nbr, f1, lo, up, *weights)
    ret1 = coarse(vec1, sums0, *(shifted(sums0, "grp", k) for k in range(1, ng)))

    (send,) = next_rhs(coarse_pick, cpos, nbr, ret1, widths[1], paf1, h, ng)
    vec2 = exchange(send)
    w1, r1, f2, sums1, sent = image_of(
        1, cpos, nbr, [ret1], widths[1:2], g, af1, right_side, w0, intersection_send, factors
    )
    lo, up = both_ways(sent)
    (af2,) = operator(nbr, f2, lo, up, *weights, paf=False)
    ret2 = coarse(vec2)

    y1, r1, sums = image_of(
        2, cpos, nbr, [ret1, ret2], widths[1:], g, af2, r1, w1, before=sums1, everyone=ns * ng
    )
    sums = lax.all_to_all(sums, ("grp", "sub"), split_axis=0, concat_axis=0, tiled=True)
    return final(cpos, sums, (ret0, ret1, ret2), widths, prolong, (f0, f1, f2), w1, r1, y1)


def solution(mesh):
    return jax.shard_map(
        local,
        mesh=mesh,
        in_specs=(
            P(("sub", "grp"), None, None),
            P(("sub", "grp"), None, None),
            P(("sub", "grp"), None, None, None),
            P(("sub", "grp"), None, None),
            P(("sub", "grp"), None, None),
            P("sub", "grp", None),
            P(("sub", "grp")),
            P(("sub", "grp"), None),
            P(("sub", "grp")),
        ),
        out_specs=(P(("sub", "grp"), None, None), P(("sub", "grp"), None, None)),
        check_vma=False,
    )
```

```python
import functools

import jax
import jax.numpy as jnp
from jax import lax
from jax.experimental import pallas as pl
from jax.experimental.pallas import tpu as pltpu
from jax.sharding import PartitionSpec as P

F32 = jnp.float32
BF16 = jnp.bfloat16
TILES = 6
MIB = 1024 * 1024
CHUNK = 8
AHEAD = 2


def nn(a, b):
    return lax.dot_general(a, b, (((1,), (0,)), ((), ())), preferred_element_type=F32)


def nt(a, b):
    return lax.dot_general(a, b, (((1,), (1,)), ((), ())), preferred_element_type=F32)


def tn(a, b):
    return lax.dot_general(a, b, (((0,), (0,)), ((), ())), preferred_element_type=F32)


def parts(x):
    head = x.astype(BF16)
    return head, (x - head.astype(F32)).astype(BF16)


def wide(x):
    return jnp.concatenate(parts(x), axis=1)


def fold(x):
    half = x.shape[1] // 2
    return x[:, :half] + x[:, half:]


def weights_nt(w):
    h, l = parts(w)
    return jnp.concatenate([jnp.concatenate([h, h], 1), jnp.concatenate([l, l], 1)], 0)


def weights_nn(w):
    h, l = parts(w)
    row = jnp.concatenate([h, l], 1)
    return jnp.concatenate([row, row], 0)


def rows_by(p):
    return weights_nt(p)


def fold_rows(x):
    half = x.shape[0] // 2
    return x[:half] + x[half:]


def cost(flops, nbytes):
    return pl.CostEstimate(flops=int(flops), bytes_accessed=int(nbytes), transcendentals=0)


SMEM = pl.BlockSpec(memory_space=pltpu.SMEM)
HBM = pl.BlockSpec(memory_space=pltpu.HBM)
INVMEM = pl.BlockSpec(memory_space=pltpu.VMEM)


def shape_of(shape, kind=F32):
    return jax.ShapeDtypeStruct(shape, kind)


def call(kernel, name, arrays, in_specs, outs, out_specs, flops, scratch=(), limit=58):
    moved = sum(x.nbytes for x in arrays) + sum(x.size * x.dtype.itemsize for x in outs)
    return pl.pallas_call(
        kernel,
        in_specs=in_specs,
        out_specs=out_specs,
        out_shape=outs,
        scratch_shapes=list(scratch),
        compiler_params=pltpu.CompilerParams(vmem_limit_bytes=limit * MIB),
        cost_estimate=cost(flops, moved),
        name=name,
    )(*arrays)


def chunk(src, dst, sems, i):
    at = pl.ds(i * CHUNK, CHUNK)
    return pltpu.make_async_copy(src.at[at], dst.at[at], sems.at[i])


def loop(count, body):
    def one(i, _):
        body(i)
        return 0

    lax.fori_loop(0, count, one, 0)


def stacked(c):
    h = c.astype(BF16).astype(F32)
    pad = jnp.zeros((-3 * c.shape[0] % 16, c.shape[1]), F32)
    return jnp.concatenate([h, c - h, h, pad], axis=0).astype(BF16)


def correction(ret, width, t):
    at = lax.div(t, TILES) * width + lax.rem(t, TILES)
    return jnp.concatenate([ret[at], ret[at + 1]], axis=1)


def gathered(find, cpos, nbr, n):
    tiles = []
    for k in range(5):
        tiles.append(find(cpos[n] if k == 0 else cpos[nbr[n * 4 + k - 1]]))
    return stacked(jnp.concatenate(tiles, axis=0))


def alpha_of(ret):
    width = TILES + 1
    total = ret[TILES]
    for q in range(1, ret.shape[0] // width):
        total = total + ret[q * width + TILES]
    return total[0:1, 0:1] / total[1:2, 0:1]


def invert(pick, inv):
    def put(q, _):
        inv[pick[q]] = q
        return 0

    lax.fori_loop(0, pick.shape[0], put, 0)


def first_kernel(pick, r_ref, p_ref, send_ref, inv_ref, r, slots, sems, out_sems):
    nb = r.shape[0]
    for i in range(nb // CHUNK):
        chunk(r_ref, r, sems, i).start()
    invert(pick, inv_ref)

    def some(i):
        chunk(r_ref, r, sems, i).wait()
        for j in range(CHUNK):
            n = i * CHUNK + j
            slots[inv_ref[n]] = fold_rows(nt(rows_by(p_ref[n]), wide(r[n])))

    loop(nb // CHUNK, some)
    copies = [
        pltpu.make_async_copy(slots, send_ref.at[g], out_sems.at[g])
        for g in range(send_ref.shape[0])
    ]
    for c in copies:
        c.start()
    for c in copies:
        c.wait()


def first_rhs(pick, r, p, groups):
    nb, nr, b = r.shape
    nc = p.shape[1]
    return call(
        first_kernel,
        "first_rhs",
        [pick, r, p],
        [SMEM, HBM, INVMEM],
        [shape_of((groups, nb, nc, nr)), shape_of((nb,), jnp.int32)],
        [HBM, SMEM],
        2 * 16 * 256 * 256 * nb,
        [
            pltpu.VMEM(r.shape, F32),
            pltpu.VMEM((nb, nc, nr), F32),
            pltpu.SemaphoreType.DMA((nb // CHUNK,)),
            pltpu.SemaphoreType.DMA((groups,)),
        ],
    )


def fine_block(v, f):
    inner = fold(nn(wide(v), weights_nn(f)))
    return fold(nt(wide(inner), weights_nt(f)))


def fine_first_kernel(send, inv, v_hbm, fac_hbm, p_ref, f_hbm, out_ref, v, fac, ext, v_sem, fac_sem, f_sem):
    steps = v.shape[0] // CHUNK
    nr = v.shape[1]
    nc = p_ref.shape[1]
    for i in range(steps):
        chunk(v_hbm, v, v_sem, i).start()
        chunk(fac_hbm, fac, fac_sem, i).start()

    def some(i):
        chunk(v_hbm, v, v_sem, i).wait()
        chunk(fac_hbm, fac, fac_sem, i).wait()
        for j in range(CHUNK):
            n = i * CHUNK + j
            ext[n] = wide(fine_block(v[n], fac[n]))
        chunk(ext, f_hbm, f_sem, i).start()

    loop(steps, some)
    for j in range(send.shape[0]):
        n = send[j]
        out_ref[j, :nr] = fold(ext[n].astype(F32))
        out_ref[j, nr : nr + nc] = p_ref[n]
        out_ref[j, nr + nc :] = jnp.full((8, p_ref.shape[2]), inv[n].astype(F32))
    for i in range(steps):
        chunk(ext, f_hbm, f_sem, i).wait()


def fine_first(send, inv, v, fac, p):
    nb, nr, b = v.shape
    nc = p.shape[1]
    return call(
        fine_first_kernel,
        "fine_first",
        [send, inv, v, fac, p],
        [SMEM, SMEM, HBM, HBM, INVMEM],
        [shape_of((nb, nr, 2 * b), BF16), shape_of((send.shape[0], nr + nc + 8, b))],
        [HBM, INVMEM],
        4 * 256**3 * nb,
        [
            pltpu.VMEM(v.shape, F32),
            pltpu.VMEM(fac.shape, F32),
            pltpu.VMEM((nb, nr, 2 * b), BF16),
        ]
        + [pltpu.SemaphoreType.DMA((nb // CHUNK,))] * 3,
    )


def operator_kernel(nbr, f_hbm, lo_ref, up_ref, d_hbm, w_hbm, p_ref, *refs, setup, paf):
    refs = list(refs)
    af_hbm = refs.pop(0)
    paf_ref = refs.pop(0) if paf else None
    if setup:
        g_ref, h_ref, pext, grows = refs[:2] + refs[-2:]
        refs = refs[2:-2]
    d, w, ext, kept, d_sem, w_sem, f_sem, af_sem = refs
    nb, nr, b = kept.shape
    nc = p_ref.shape[1]
    halo = lo_ref.shape[0]
    steps = nb // CHUNK

    for i in range(steps):
        chunk(f_hbm, ext, f_sem, i).start()

    def fetch(i):
        chunk(d_hbm, d, d_sem, i).start()
        chunk(w_hbm, w, w_sem, i).start()

    for i in range(AHEAD):
        fetch(i)
    for j in range(halo):
        ext[nb + j] = wide(lo_ref[j, :nr])
        ext[nb + halo + j] = wide(up_ref[j, :nr])
    if setup:
        pext[pl.ds(0, nb)] = p_ref[...]
        pext[pl.ds(nb, halo)] = lo_ref[:, nr : nr + nc]
        pext[pl.ds(nb + halo, halo)] = up_ref[:, nr : nr + nc]
    for i in range(steps):
        chunk(f_hbm, ext, f_sem, i).wait()

    def products(i):
        for j in range(CHUNK):
            n = i * CHUNK + j
            p = p_ref[n]
            paf_ref[n] = fold_rows(nt(wide(kept[n]), rows_by(p)).T)
            if setup:
                g = grows[n]
                gh = g.astype(BF16).astype(F32)
                pad = jnp.zeros((8, g.shape[1]), F32)
                g_ref[n] = jnp.concatenate([gh, gh, g - gh, pad], axis=0).astype(BF16)
                thrice = jnp.concatenate([g, g, g, pad], axis=0)
                h = fold_rows(nt(rows_by(p), wide(thrice)))
                hh = h.astype(BF16).astype(F32)
                lane = lax.broadcasted_iota(jnp.int32, h.shape, 1)
                h_ref[n] = jnp.where(lane < 80, hh, h - hh)

    def image(i):
        chunk(d_hbm, d, d_sem, i).wait()
        chunk(w_hbm, w, w_sem, i).wait()
        if i + AHEAD < steps:
            fetch(i + AHEAD)
        if paf and i:
            products(i - 1)
        for j in range(CHUNK):
            n = i * CHUNK + j
            fields = []
            weights = []
            rows = []
            for k in range(5):
                e = n if k == 0 else nbr[n * 4 + k - 1]
                weights.append(weights_nt(d[n] if k == 0 else w[n, k - 1]))
                fields.append(ext[e])
                if setup:
                    p = pext[e]
                    ph = p.astype(BF16).astype(F32)
                    row = [jnp.zeros((nc, 2 * b), F32)] * 5
                    row[k] = jnp.concatenate([ph, p - ph], axis=1)
                    rows.append(jnp.concatenate(row, axis=1))
            lhs = jnp.concatenate(fields, axis=1)
            if setup:
                rows = jnp.concatenate(rows + [jnp.zeros_like(rows[0])], axis=0).astype(BF16)
                lhs = jnp.concatenate([lhs, rows], axis=0)
            got = fold(nt(lhs, jnp.concatenate(weights, axis=1)))
            if setup:
                grows[n] = got[nr : nr + 5 * nc]
                got = got[:nr]
            kept[n] = got
        chunk(kept, af_hbm, af_sem, i).start()

    for i in range(steps):
        image(i)
    if paf:
        products(steps - 1)
    for i in range(steps):
        chunk(kept, af_hbm, af_sem, i).wait()


def operator(nbr, f, lo, up, d, w, p, setup=False, paf=True):
    nb, nc, b = p.shape
    nr = f.shape[1]
    places = nb + 2 * lo.shape[0]
    outs = [shape_of((nb, nr, b))]
    scratch = [pltpu.VMEM(d.shape, F32), pltpu.VMEM(w.shape, F32)]
    scratch += [pltpu.VMEM((places, nr, 2 * b), BF16), pltpu.VMEM((nb, nr, b), F32)]
    scratch += [pltpu.SemaphoreType.DMA((nb // CHUNK,))] * 4
    if paf:
        outs.append(shape_of((nb, nc, nr)))
    if setup:
        outs += [shape_of((nb, b, b), BF16), shape_of((nb, nc, b))]
        scratch += [pltpu.VMEM((places, nc, b), F32), pltpu.VMEM((nb, 5 * nc, b), F32)]
    return call(
        functools.partial(operator_kernel, setup=setup, paf=paf),
        "operator",
        [nbr, f, lo, up, d, w, p],
        [SMEM, HBM, INVMEM, INVMEM, HBM, HBM, INVMEM],
        outs,
        [HBM] + [INVMEM] * (len(outs) - 1),
        10 * 256**3 * nb,
        scratch,
        53,
    )


def solve_kernel(v_ref, c_ref, *refs):
    *sums, out_ref, res, sem = refs
    vh, vl = parts(v_ref[...])
    ch, cl = parts(c_ref[0])
    sol = nn(ch, vh) + nn(ch, vl) + nn(cl, vh)
    ns = res.shape[0]
    half = sol.shape[1] // 2
    if sums:
        total = sums[0][...] + sums[1][...] + sums[2][...] + sums[3][...]
    for s in range(ns):
        rows = sol[8 * s : 8 * s + 8]
        for place, to in ((0, s), (1, (s + 1) % ns), (2, (s - 1) % ns)):
            res[to, 2 * place] = rows[:, :half]
            res[to, 2 * place + 1] = rows[:, half:]
        if sums:
            res[s, TILES] = total
    out = pltpu.make_async_copy(res, out_ref, sem)
    out.start()
    out.wait()


def solve(vec, inverse, ns, sums):
    k, nr = vec.shape
    shape = (ns, TILES + (1 if sums else 0), 8, nr // 2)
    return call(
        solve_kernel,
        "coarse_solve",
        [vec, inverse, *sums],
        [INVMEM, INVMEM] + [INVMEM] * len(sums),
        [shape_of(shape)],
        [HBM],
        2 * 3 * 256 * k * nr,
        [pltpu.VMEM(shape, F32), pltpu.SemaphoreType.DMA],
        24,
    )[0]


def next_kernel(pick, cpos, nbr, ret_ref, paf_ref, h_ref, *refs, width):
    nb = paf_ref.shape[0]
    send_ref, slots, sems = refs
    groups = send_ref.shape[0]

    def out(i, g):
        at = pl.ds(i * CHUNK, CHUNK)
        return pltpu.make_async_copy(slots.at[at], send_ref.at[g, at], sems.at[g, i])

    def some(i):
        for j in range(CHUNK):
            q = i * CHUNK + j
            n = pick[q]
            c = gathered(lambda t: correction(ret_ref, width, t), cpos, nbr, n)
            slots[q] = paf_ref[n] + nn(h_ref[n].astype(BF16), c)
        for g in range(groups):
            out(i, g).start()

    loop(nb // CHUNK, some)
    for i in range(nb // CHUNK):
        for g in range(groups):
            out(i, g).wait()


def next_rhs(pick, cpos, nbr, ret, width, paf, h, groups):
    nb, nc, nr = paf.shape
    return call(
        functools.partial(next_kernel, width=width),
        "next_rhs",
        [pick, cpos, nbr, ret, paf, h],
        [SMEM] * 3 + [INVMEM] * 3,
        [shape_of((groups, nb, nc, nr))],
        [HBM],
        2 * 16 * 256 * 128 * nb,
        [pltpu.VMEM((nb, nc, nr), F32), pltpu.SemaphoreType.DMA((groups, nb // CHUNK))],
        24,
    )


def image_kernel(cpos, nbr, *refs, stage, widths):
    refs = list(refs)

    def take(count):
        found = refs[:count]
        del refs[:count]
        return found

    send = None if stage == 2 else refs.pop(0)
    rets = take(2 if stage == 2 else 1)
    g_hbm, af_hbm, r_hbm = take(3)
    old_hbm = refs.pop(0) if stage else None
    fac_hbm = None if stage == 2 else refs.pop(0)
    before_ref = refs.pop(0) if stage == 2 else None
    w_out = refs.pop(0)
    r_out = refs.pop(0) if stage == 1 else None
    if stage == 2:
        kept_r = refs.pop(0)
    f_out = None if stage == 2 else refs.pop(0)
    sum_ref = refs.pop(0)
    sent_ref = None if stage == 2 else refs.pop(0)
    if stage == 2:
        af, r = w_out, kept_r
        g, old, af_sem, r_sem, g_sem, old_sem = take(6)
    else:
        af, r, g, af_sem, r_sem, g_sem, w_sem = take(7)
        if stage:
            old, old_sem = take(2)
    if stage < 2:
        fac, ext, fac_sem, r_out_sem, f_sem = take(5)
    nb = af.shape[0]
    steps = nb // CHUNK

    def ins(i):
        found = [chunk(af_hbm, af, af_sem, i), chunk(r_hbm, r, r_sem, i), chunk(g_hbm, g, g_sem, i)]
        if stage:
            found.append(chunk(old_hbm, old, old_sem, i))
        if stage < 2:
            found.append(chunk(fac_hbm, fac, fac_sem, i))
        return found

    def outs(i):
        if stage == 2:
            return []
        found = [chunk(af, w_out, w_sem, i)]
        if stage == 1:
            found.append(chunk(r, r_out, r_out_sem, i))
        return found

    for i in range(steps):
        for c in ins(i):
            c.start()
    alpha = alpha_of(rets[0]) if stage else None

    def find(t):
        c = correction(rets[0], widths[0], t)
        if stage == 2:
            c = c - alpha * correction(rets[1], widths[1], t)
        return c

    def fine(i):
        for j in range(CHUNK):
            n = i * CHUNK + j
            ext[n] = wide(fine_block(af[n], fac[n]))
        chunk(ext, f_out, f_sem, i).start()

    def some(i, acc):
        acc = list(acc)
        for c in ins(i):
            c.wait()
        for j in range(CHUNK):
            n = i * CHUNK + j
            w = af[n] + tn(gathered(find, cpos, nbr, n), g[n])
            res = r[n]
            if stage == 0:
                pairs = ((w, res), (w, w))
            elif stage == 1:
                before = old[n]
                w = before - alpha * w
                res = res - alpha * before
                r[n] = res
                pairs = ((w, res), (w, w))
            else:
                pairs = ((w, res), (w, w), (w, old[n]))
            af[n] = w
            for k, (x, y) in enumerate(pairs):
                acc[k] += jnp.sum((x * y).reshape(-1, 8, w.shape[1]), axis=0)
        if stage < 2 and i:
            fine(i - 1)
        for c in outs(i):
            c.start()
        return acc

    zero = jnp.zeros((8, af.shape[2]), F32)
    acc = [zero] * (3 if stage == 2 else 2)
    for i in range(steps):
        acc = some(i, acc)
    acc = [jnp.sum(x, keepdims=True) for x in acc]
    shape = (2, af.shape[2]) if stage == 2 else sum_ref.shape
    row = lax.broadcasted_iota(jnp.int32, shape, 1 if stage == 2 else 0)
    if stage == 2:
        acc += [before_ref[0:1, 0:1], before_ref[1:2, 0:1]]
    total = jnp.zeros(shape, F32)
    for k, x in enumerate(acc):
        total = jnp.where(row == k, x, total)
    if stage == 2:
        for k in range(sum_ref.shape[0]):
            sum_ref[k] = total
    else:
        sum_ref[...] = total
        fine(steps - 1)
        for j in range(send.shape[0]):
            sent_ref[j] = fold(ext[send[j]].astype(F32))
        for i in range(steps):
            chunk(ext, f_out, f_sem, i).wait()
    for i in range(steps):
        for c in outs(i):
            c.wait()


def image_of(stage, cpos, nbr, rets, widths, g, af, r, old=None, send=None, fac=None, before=None, everyone=0):
    nb, nr, b = af.shape
    steps = nb // CHUNK
    dma = pltpu.SemaphoreType.DMA
    ins = [cpos, nbr] + ([] if send is None else [send])
    specs = [SMEM] * len(ins)
    ins += [*rets, g, af, r]
    specs += [INVMEM] * len(rets) + [HBM] * 3
    scratch = [pltpu.VMEM(g.shape, BF16)]
    if stage < 2:
        scratch = [pltpu.VMEM(af.shape, F32)] * 2 + scratch
    else:
        scratch.append(pltpu.VMEM(af.shape, F32))
    scratch += [dma((steps,))] * 4
    if stage:
        ins.append(old)
        specs.append(HBM)
    if stage == 1:
        scratch += [pltpu.VMEM(af.shape, F32), dma((steps,))]
    outs = [shape_of(af.shape)] * (2 if stage else 1)
    if stage < 2:
        outs.append(shape_of((nb, nr, 2 * b), BF16))
    out_specs = [HBM if stage < 2 else INVMEM] * len(outs)
    if stage < 2:
        count = send.shape[0]
        ins.append(fac)
        specs.append(HBM)
        outs += [shape_of((8, b)), shape_of((count, nr, b))]
        scratch += [pltpu.VMEM(fac.shape, F32), pltpu.VMEM((nb, nr, 2 * b), BF16)]
        scratch += [dma((steps,))] * 3
    else:
        ins.append(before)
        specs.append(INVMEM)
        outs.append(shape_of((everyone, 2, b)))
    out_specs += [INVMEM] * (len(outs) - len(out_specs))
    return call(
        functools.partial(image_kernel, stage=stage, widths=widths),
        "image",
        ins,
        specs,
        outs,
        out_specs,
        2 * 256 * 128 * 128 * nb,
        scratch,
        58 if stage < 2 else 48,
    )


def final_kernel(cpos, *refs, widths):
    sum_ref, rets, p_ref = refs[0], refs[1:4], refs[4]
    hbms, (r, y), (s_hbm, r_hbm) = refs[5:9], refs[9:11], refs[11:13]
    s, res, *refs = refs[13:]
    bufs, (s_sem, r_sem), sems = refs[:4], refs[4:6], refs[6:]
    fs, w = bufs[:3], bufs[3]
    nb = p_ref.shape[0]
    for i in range(nb // CHUNK):
        for k in range(4):
            chunk(hbms[k], bufs[k], sems[k], i).start()
    total = jnp.sum(sum_ref[...], axis=0)
    yr, yy, yw, wr, ww = (total[0:1, k : k + 1] for k in range(5))
    a0 = alpha_of(rets[1])
    a1 = wr / ww
    a2 = (wr - a1 * ww - a1 * yr + a1 * a1 * yw) / (ww - 2.0 * a1 * yw + a1 * a1 * yy)
    b0 = a0 + a1 + a2
    b1 = -a0 * (a1 + a2)
    b2 = -a1 * a2

    def some(i):
        for k in range(4):
            chunk(hbms[k], bufs[k], sems[k], i).wait()
        for j in range(CHUNK):
            n = i * CHUNK + j
            p = p_ref[n]
            ph = p.astype(BF16).astype(F32)
            p3 = jnp.concatenate([ph, ph, p - ph, jnp.zeros_like(p)], axis=0).astype(BF16)
            c0, c1, cy = (correction(x, k, cpos[n]) for x, k in zip(rets, widths))
            c = b0 * c0 + (b1 + b2) * c1 - b2 * a0 * cy
            f0, f1, f2 = (fold(x[n].astype(F32)) for x in fs)
            s[n] = b0 * f0 + b1 * f1 + b2 * f2 + tn(stacked(c), p3)
            res[n] = r[n] - (a1 + a2) * w[n] + a1 * a2 * y[n]
        chunk(s, s_hbm, s_sem, i).start()
        chunk(res, r_hbm, r_sem, i).start()

    loop(nb // CHUNK, some)
    for i in range(nb // CHUNK):
        chunk(s, s_hbm, s_sem, i).wait()
        chunk(res, r_hbm, r_sem, i).wait()


def final(cpos, sums, rets, widths, p, fs, w, r, y):
    nb = p.shape[0]
    return call(
        functools.partial(final_kernel, widths=widths),
        "final",
        [cpos, sums, *rets, p, *fs, w, r, y],
        [SMEM] + [INVMEM] * 5 + [HBM] * 4 + [INVMEM] * 2,
        [shape_of(w.shape)] * 2,
        [HBM, HBM],
        2 * 256 * 128 * 128 * nb,
        [pltpu.VMEM(w.shape, F32)] * 2
        + [pltpu.VMEM(x.shape, x.dtype) for x in (*fs, w)]
        + [pltpu.SemaphoreType.DMA((nb // CHUNK,))] * 6,
        42,
    )


def shifted(x, axis, by):
    count = lax.axis_size(axis)
    return lax.ppermute(x, axis, [(i, (i + by) % count) for i in range(count)])


def both_ways(x):
    return shifted(x, "sub", 1), shifted(x, "sub", -1)


def local(
    right_side,
    diag_blocks,
    couplings,
    factors,
    prolong,
    coarse_inverse,
    intersection_send,
    neighbours,
    coarse_pick,
):
    nb, nr, b = right_side.shape
    nc = prolong.shape[1]
    ns = lax.axis_size("sub")
    ng = lax.axis_size("grp")
    nbr = neighbours.reshape(-1)

    def exchange(send):
        flat = send.reshape(ng * nb, nc, nr)
        got = lax.all_to_all(flat, ("grp", "sub"), split_axis=0, concat_axis=0, tiled=True)
        return got.reshape(ng * nb * nc, nr)

    def coarse(vec, *sums):
        out = solve(vec, coarse_inverse, ns, sums)
        back = lax.all_to_all(out, "sub", split_axis=0, concat_axis=0, tiled=True)
        return back.reshape(-1, 8, nr // 2)

    def places(x):
        return x[:, nr + nc, 0].astype(jnp.int32) * TILES

    weights = (diag_blocks, couplings, prolong)
    widths = (TILES, TILES + 1, TILES)
    send, inv = first_rhs(coarse_pick, right_side, prolong, ng)
    vec0 = exchange(send)
    f0, sent = fine_first(intersection_send, inv, right_side, factors, prolong)
    lo, up = both_ways(sent)
    cpos = jnp.concatenate([inv * TILES, places(lo) + 2, places(up) + 4])
    af0, paf0, g, h = operator(nbr, f0, lo, up, *weights, setup=True)
    ret0 = coarse(vec0)

    (send,) = next_rhs(coarse_pick, cpos, nbr, ret0, widths[0], paf0, h, ng)
    vec1 = exchange(send)
    w0, f1, sums0, sent = image_of(
        0, cpos, nbr, [ret0], widths[:1], g, af0, right_side, send=intersection_send, fac=factors
    )
    lo, up = both_ways(sent)
    af1, paf1 = operator(nbr, f1, lo, up, *weights)
    ret1 = coarse(vec1, sums0, *(shifted(sums0, "grp", k) for k in range(1, ng)))

    (send,) = next_rhs(coarse_pick, cpos, nbr, ret1, widths[1], paf1, h, ng)
    vec2 = exchange(send)
    w1, r1, f2, sums1, sent = image_of(
        1, cpos, nbr, [ret1], widths[1:2], g, af1, right_side, w0, intersection_send, factors
    )
    lo, up = both_ways(sent)
    (af2,) = operator(nbr, f2, lo, up, *weights, paf=False)
    ret2 = coarse(vec2)

    y1, r1, sums = image_of(
        2, cpos, nbr, [ret1, ret2], widths[1:], g, af2, r1, w1, before=sums1, everyone=ns * ng
    )
    sums = lax.all_to_all(sums, ("grp", "sub"), split_axis=0, concat_axis=0, tiled=True)
    return final(cpos, sums, (ret0, ret1, ret2), widths, prolong, (f0, f1, f2), w1, r1, y1)


def solution(mesh):
    return jax.shard_map(
        local,
        mesh=mesh,
        in_specs=(
            P(("sub", "grp"), None, None),
            P(("sub", "grp"), None, None),
            P(("sub", "grp"), None, None, None),
            P(("sub", "grp"), None, None),
            P(("sub", "grp"), None, None),
            P("sub", "grp", None),
            P(("sub", "grp")),
            P(("sub", "grp"), None),
            P(("sub", "grp")),
        ),
        out_specs=(P(("sub", "grp"), None, None), P(("sub", "grp"), None, None)),
        check_vma=False,
    )
```
